32 devices in a mesh: dp: 4 (over y, core), seq: 8 (over z, x).
Axes of the slice: x: 2, y: 2, z: 4, core: 2. Of those that a mesh axis runs over, the one named last changes fastest.
Arguments:
- queries: bfloat16 [4096, 2560], P(('dp', 'seq')), may hold values from -10 to 10
- key_rows: bfloat16 [4096, 512], P(('dp', 'seq')), may hold values from -10 to 10
- value_rows: bfloat16 [4096, 512], P(('dp', 'seq')), may hold values from -6 to 6
- grad_out: bfloat16 [4096, 2560], P(('dp', 'seq')), may hold values from -6 to 6
- segments: int32 [4, 1024], P('dp', 'seq'), may hold values from 0 to 3, never falling along the last dimension, each value on 1 to 512 neighbouring positions
- layer_input: bfloat16 [4096, 5120], P(('dp', 'seq')), may hold values from -6 to 6
Outputs:
- grad_queries: bfloat16 [4096, 2560], P(('dp', 'seq'))
- grad_keys: bfloat16 [4096, 512], P(('dp', 'seq'))
- grad_values: bfloat16 [4096, 512], P(('dp', 'seq'))
- grad_key_weight: float32 [5120, 512], P(('dp', 'seq'))
The draws below stay inside these ranges and needn't reach their ends.
Inputs may be any that keep to these rules, and one draw needn't show every extreme that they name: `segments`: within each row the ids never fall, each sequence holds 1 to 512 tokens, and one holds exactly 512.
All inputs are finite; a program needn't handle non-finite values.
Results may differ from the reference program's by a relative error of at most 0.0082.
Values may be sent and summed in bfloat16 or wider, within the bound.
A program may use at most 128 MiB of HBM per device.

```python
import math
import jax
import jax.numpy as jnp
import numpy as np
from jax import lax

D = 5120
HQ = 20
HK = 4
HD = 128
ROW_TOK = 1024
TOKENS = 4096
MOST = 512
SEGS = 4
N_DP = 4


def draw_key_rows(key, part):
    key = jax.random.fold_in(key, 5)
    values = jnp.clip(jax.random.normal(key, (TOKENS, HK * HD), jnp.float32), -6.0, 6.0)
    return values.astype(jnp.bfloat16)


def draw_queries(key, part):
    key = jax.random.fold_in(key, 7)
    values = jnp.clip(jax.random.normal(key, (TOKENS, HQ * HD), jnp.float32), -6.0, 6.0)
    return values.astype(jnp.bfloat16)


def with_spikes(values, key, source, target, parts, factor):
    def block_of(position):
        return (jnp.arange(values.shape[position]) // (values.shape[position] // parts)).reshape((-1,) + (1,) * (values.ndim - 1 - position))

    near = jax.random.permutation(key, parts)[block_of(target)]
    other_side = (block_of(target) + parts // 2) % parts
    return jnp.where((block_of(source) == near) | (block_of(source) == other_side), factor * values, values)


def block_levels(key, extent, cuts, low, largest):
    def one(position, shards_of):
        draws = jax.random.uniform(jax.random.fold_in(jax.random.fold_in(key, 6), position), (shards_of,), jnp.float32, low / len(cuts), largest / len(cuts))
        return jnp.repeat(jnp.exp(draws), extent[position] // shards_of).reshape((-1,) + (1,) * (len(extent) - position - 1))

    loudness = one(*cuts[0])
    for cut in cuts[1:]:
        loudness = loudness * one(*cut)
    return loudness


def split_up(count, total, bound, skew):
    portions = [(1 << 20) // math.isqrt(grade ** skew) + 1 for grade in range(2, count + 1)]
    spare, holding = total - bound - (count - 1), [1] * (count - 1)
    while spare > 0:
        candidates = [i for i in range(count - 1) if holding[i] < bound]
        whole, budget = sum([portions[i] for i in candidates]), spare
        for i in candidates:
            addition = min(bound - holding[i], max(1, budget * portions[i] // whole), spare)
            holding[i] = holding[i] + addition
            spare = spare - addition
    return np.array([bound] + holding)


def ragged(rng, amount, total, reach, skew):
    if amount == 2:
        one = jax.random.randint(rng, (), max(1, total - reach), min(reach, total - 1) + 1)
        return jnp.stack([one, total - one])
    lengths = jnp.asarray(split_up(amount, total, reach, skew), jnp.int32)
    twos = (amount - 1) // 2
    donor, taker = lengths[1:1 + 2 * twos:2], lengths[2:2 + 2 * twos:2]
    margin = jnp.minimum(donor - 1, reach - taker)
    shifted = jax.random.randint(jax.random.fold_in(rng, 1), (twos,), 0, 1 << 20) % (margin + 1)
    lengths = lengths.at[1:1 + 2 * twos:2].set(donor - shifted).at[2:2 + 2 * twos:2].set(taker + shifted)
    return lengths[jax.random.permutation(jax.random.fold_in(rng, 2), amount)]


def bell_draw(own_key, extent, deviation, limit, shards=(), kind=jnp.bfloat16):
    array = jax.random.normal(own_key, extent, jnp.float32) * deviation
    if len(shards) > 0:
        array = block_levels(own_key, extent, shards, -0.22, 0.18) * array
    return jnp.clip(array, min=-limit, max=limit).astype(kind)


def heavy_noise(key, extent, deviation, bound, shards, heavy, dtype=jnp.bfloat16):
    result = deviation * jax.random.normal(key, extent, jnp.float32)
    if shards:
        result = result * block_levels(key, extent, shards, -0.22, 0.18)
    return jnp.clip(with_spikes(result, jax.random.fold_in(key, 3), *heavy), -bound, bound).astype(dtype)


def setup_inputs(seed: int = 0) -> dict:
    splits = jax.random.split(jax.random.key(seed), 7)
    return {
        "queries": draw_queries(jax.random.fold_in(splits[6], 71), 0),
        "key_rows": draw_key_rows(jax.random.fold_in(splits[6], 71), 0),
        "value_rows": bell_draw(splits[2], (TOKENS, HK * HD), 1.0, 6.0, ((0, 32),)),
        "grad_out": bell_draw(splits[3], (TOKENS, HQ * HD), 1.0, 6.0, ((0, 32),)),
        "segments": jax.vmap(lambda own: jnp.searchsorted(jnp.cumsum(ragged(own, SEGS, ROW_TOK, MOST, 1)), jnp.arange(ROW_TOK), side="right"))(jax.random.split(splits[4], N_DP)).reshape((N_DP, ROW_TOK)).astype(jnp.int32),
        "layer_input": heavy_noise(splits[5], (TOKENS, D), 1.0, 6.0, ((0, 32),), (0, 1, 32, 2.75)),
    }


def row_backward(packed):
    query_block, key_block, value_block, grad_block, seg_row = packed
    length = query_block.shape[0]
    repeat = HQ // HK
    scaling = HD ** -0.5
    places = jnp.arange(length)
    visible = (seg_row[:, None] == seg_row[None, :]) & (places[None, :] <= places[:, None])
    grads_q, grads_k, grads_v = [], [], []
    for g in range(HK):
        query_group = query_block[:, g * repeat * HD:(g + 1) * repeat * HD].reshape(length, repeat, HD).astype(jnp.float32)
        grad_group = grad_block[:, g * repeat * HD:(g + 1) * repeat * HD].reshape(length, repeat, HD).astype(jnp.float32)
        key_head = key_block[:, g * HD:(g + 1) * HD].astype(jnp.float32)
        value_head = value_block[:, g * HD:(g + 1) * HD].astype(jnp.float32)
        logits = jnp.einsum("ird,jd->rij", query_group, key_head) * scaling
        logits = jnp.where(visible[None], logits, -1e30)
        top = jnp.max(logits, axis=-1, keepdims=True)
        raised = jnp.where(visible[None], jnp.exp(logits - top), 0.0)
        probs = raised / jnp.sum(raised, axis=-1, keepdims=True)
        grad_probs = jnp.einsum("ird,jd->rij", grad_group, value_head)
        delta = jnp.sum(probs * grad_probs, axis=-1, keepdims=True)
        grad_logits = probs * (grad_probs - delta) * scaling
        probs_low = lax.optimization_barrier(probs.astype(jnp.bfloat16)).astype(jnp.float32)
        grad_low = lax.optimization_barrier(grad_logits.astype(jnp.bfloat16)).astype(jnp.float32)
        grads_q.append(jnp.einsum("rij,jd->ird", grad_low, key_head).reshape(length, repeat * HD))
        grads_k.append(jnp.einsum("rij,ird->jd", grad_low, query_group))
        grads_v.append(jnp.einsum("rij,ird->jd", probs_low, grad_group))
    return (jnp.concatenate(grads_q, axis=1).astype(jnp.bfloat16),
            jnp.concatenate(grads_k, axis=1).astype(jnp.bfloat16),
            jnp.concatenate(grads_v, axis=1).astype(jnp.bfloat16))


def reference(queries, key_rows, value_rows, grad_out, segments, layer_input):
    rows = segments.shape[0]
    packed = (queries.reshape(rows, ROW_TOK, HQ * HD), key_rows.reshape(rows, ROW_TOK, HK * HD),
              value_rows.reshape(rows, ROW_TOK, HK * HD), grad_out.reshape(rows, ROW_TOK, HQ * HD), segments)
    grad_q, grad_k, grad_v = lax.map(row_backward, packed)
    grad_q = grad_q.reshape(TOKENS, HQ * HD)
    grad_k = grad_k.reshape(TOKENS, HK * HD)
    grad_v = grad_v.reshape(TOKENS, HK * HD)
    weight_grad = jnp.dot(layer_input.T, grad_k, preferred_element_type=jnp.float32)
    return grad_q, grad_k, grad_v, weight_grad
```

```python
import functools

import jax
import jax.numpy as jnp
from jax import lax
from jax.experimental import pallas as pl
from jax.experimental.pallas import tpu as pltpu
from jax.sharding import PartitionSpec as P

HQ = 20
HK = 4
HD = 128
REP = HQ // HK
BACK = 4
MESH = pl.DeviceIdType.MESH


def kernel(cfg, *refs):
    n_dp, n_seq, rows, fused, chunk = cfg
    n_z = n_seq // 2
    width = BACK + 1
    keys = width * rows
    refs = list(refs)
    q_ref, k_ref, v_ref, do_ref, seg_ref = refs[:5]
    del refs[:5]
    x_ref = refs.pop(0) if fused else None
    dq_ref, dk_ref, dv_ref = refs[:3]
    del refs[:3]
    dw_ref = refs.pop(0) if fused else None
    (win, segw, cont, part, accr, bias, qs, dos, dst, pst) = refs[:10]
    del refs[:10]
    (kv_s, kv_r, sg_s, sg_r, gr_s, gr_r) = refs[:6]
    del refs[:6]
    if fused:
        (xs, xr, dkg, pf, psend, prec, x_s, x_r, dk_s, dk_r, w_s, w_r) = refs
    d = lax.axis_index("dp")
    s = lax.axis_index("seq")
    z = s // 2
    x = s % 2
    me = d * 2 + x
    scale = HD ** -0.5

    plane = []
    if fused:
        for j in range(n_dp):
            for e in range(2):
                if j or e:
                    dd = (d + j) % n_dp
                    xx = (x + e) % 2
                    plane.append((dd, z * 2 + xx, dd * 2 + xx))

    barrier = pltpu.get_barrier_semaphore()
    count = 0
    for j in range(1, n_seq):
        pl.semaphore_signal(barrier, inc=1, device_id=(d, (s + j) % n_seq), device_id_type=MESH)
        count += 1
    if fused:
        for j in range(1, n_dp):
            for e in range(2):
                pl.semaphore_signal(
                    barrier, inc=1,
                    device_id=((d + j) % n_dp, z * 2 + (x + e) % 2), device_id_type=MESH,
                )
                count += 1

    for g in range(HK):
        win[g, BACK, :, :HD] = k_ref[:, g * HD:(g + 1) * HD]
        win[g, BACK, :, HD:] = v_ref[:, g * HD:(g + 1) * HD]
    segw[BACK] = jnp.broadcast_to(seg_ref[...], (8, rows))

    def kv_copy(g, k):
        return pltpu.make_async_remote_copy(
            src_ref=win.at[g, BACK], dst_ref=win.at[g, BACK - k],
            send_sem=kv_s.at[g, k - 1], recv_sem=kv_r.at[g, k - 1],
            device_id=(d, (s + k) % n_seq), device_id_type=MESH,
        )

    def seg_copy(k):
        return pltpu.make_async_remote_copy(
            src_ref=segw.at[BACK], dst_ref=segw.at[BACK - k],
            send_sem=sg_s.at[k - 1], recv_sem=sg_r.at[k - 1],
            device_id=(d, (s + k) % n_seq), device_id_type=MESH,
        )

    def grad_copy(g, k):
        return pltpu.make_async_remote_copy(
            src_ref=cont.at[g, BACK - k], dst_ref=part.at[g, k - 1],
            send_sem=gr_s.at[g, k - 1], recv_sem=gr_r.at[g, k - 1],
            device_id=(d, (s + n_seq - k) % n_seq), device_id_type=MESH,
        )

    def x_copy(i, to):
        return pltpu.make_async_remote_copy(
            src_ref=xs.at[to[2]], dst_ref=xr.at[me],
            send_sem=x_s.at[i], recv_sem=x_r.at[me],
            device_id=(to[0], to[1]), device_id_type=MESH,
        )

    def x_arrival(i, to):
        return pltpu.make_async_remote_copy(
            src_ref=xs.at[to[2]], dst_ref=xr.at[to[2]],
            send_sem=x_s.at[i], recv_sem=x_r.at[to[2]],
            device_id=(to[0], to[1]), device_id_type=MESH,
        )

    def dk_copy(g, i, to):
        return pltpu.make_async_remote_copy(
            src_ref=dkg.at[g, me], dst_ref=dkg.at[g, me],
            send_sem=dk_s.at[g, i], recv_sem=dk_r.at[g, me],
            device_id=(to[0], to[1]), device_id_type=MESH,
        )

    def dk_arrival(g, i, to):
        return pltpu.make_async_remote_copy(
            src_ref=dkg.at[g, me], dst_ref=dkg.at[g, to[2]],
            send_sem=dk_s.at[g, i], recv_sem=dk_r.at[g, to[2]],
            device_id=(to[0], to[1]), device_id_type=MESH,
        )

    def w_copy(g, j):
        zz = (z + j) % n_z
        return pltpu.make_async_remote_copy(
            src_ref=psend.at[g, zz], dst_ref=prec.at[g, z],
            send_sem=w_s.at[g, j], recv_sem=w_r.at[g, z],
            device_id=(d, zz * 2 + x), device_id_type=MESH,
        )

    def w_arrival(g, j):
        zz = (z + j) % n_z
        return pltpu.make_async_remote_copy(
            src_ref=psend.at[g, zz], dst_ref=prec.at[g, zz],
            send_sem=w_s.at[g, j], recv_sem=w_r.at[g, zz],
            device_id=(d, zz * 2 + x), device_id_type=MESH,
        )

    pl.semaphore_wait(barrier, count)

    for k in range(1, BACK + 1):
        @pl.when(s + k < n_seq)
        def _():
            seg_copy(k).start()

    for g in range(HK):
        for k in range(1, BACK + 1):
            @pl.when(s + k < n_seq)
            def _():
                kv_copy(g, k).start()

    if fused:
        for dd in range(n_dp):
            for xx in range(2):
                cols = [(dd * n_seq + 2 * zz + xx) * chunk for zz in range(n_z)]
                xs[dd * 2 + xx] = jnp.concatenate([x_ref[:, c:c + chunk] for c in cols], axis=1)
        for i, to in enumerate(plane):
            x_copy(i, to).start()
        xr[me] = xs[me]

    for k in range(1, BACK + 1):
        @pl.when(s < k)
        def _():
            win[:, BACK - k] = jnp.zeros((HK, rows, 2 * HD), jnp.bfloat16)
            bias[(BACK - k) * rows:(BACK - k + 1) * rows, :] = jnp.full((rows, rows), -1e30, jnp.float32)

    seg_here = seg_ref[...].astype(jnp.float32)

    def seg_bias(b, causal):
        there = jnp.broadcast_to(segw[b, 0:1, :].astype(jnp.float32), (rows, rows)).T
        seen = there == seg_here
        if causal:
            seen &= (lax.broadcasted_iota(jnp.int32, (rows, rows), 0)
                     <= lax.broadcasted_iota(jnp.int32, (rows, rows), 1))
        bias[b * rows:(b + 1) * rows, :] = jnp.where(seen, 0.0, -1e30)

    seg_bias(BACK, True)
    for k in range(1, BACK + 1):
        @pl.when(s >= k)
        def _():
            seg_copy(k).wait_recv()
            seg_bias(BACK - k, False)

    def attend(g):
        for k in range(1, BACK + 1):
            @pl.when(s >= k)
            def _():
                kv_copy(g, k).wait_recv()
        key = win[g, :, :, :HD].reshape(keys, HD)
        value = win[g, :, :, HD:].reshape(keys, HD)
        base = pl.multiple_of(g * (REP * HD), HD)
        for r in range(REP):
            at = pl.ds(pl.multiple_of(base + r * HD, HD), HD)
            q = q_ref[:, at]
            do = do_ref[:, at]
            qs[r * rows:(r + 1) * rows, :] = q
            dos[r * rows:(r + 1) * rows, :] = do
            nt = (((1,), (1,)), ((), ()))
            logits = lax.dot_general(key, q, nt, preferred_element_type=jnp.float32)
            gp = lax.dot_general(value, do, nt, preferred_element_type=jnp.float32)
            logits = logits * scale + bias[...]
            top = jnp.max(logits, axis=0, keepdims=True)
            raised = jnp.exp(logits - top)
            inv = 1.0 / jnp.sum(raised, axis=0, keepdims=True)
            probs = raised * inv
            delta = jnp.sum(probs * gp, axis=0, keepdims=True)
            pst[:, r * rows:(r + 1) * rows] = probs.astype(jnp.bfloat16)
            dst[:, r * rows:(r + 1) * rows] = (probs * (gp - delta) * scale).astype(jnp.bfloat16)
        dk = jnp.dot(dst[...], qs[...], preferred_element_type=jnp.float32)
        cont[g, :, :, :HD] = dk.reshape(width, rows, HD).astype(jnp.bfloat16)
        accr[g, :, :HD] = dk[BACK * rows:]
        dv = jnp.dot(pst[...], dos[...], preferred_element_type=jnp.float32)
        cont[g, :, :, HD:] = dv.reshape(width, rows, HD).astype(jnp.bfloat16)
        accr[g, :, HD:] = dv[BACK * rows:]
        for k in range(BACK, 0, -1):
            @pl.when(s >= k)
            def _():
                grad_copy(g, k).start()
        dqt = lax.dot_general(key, dst[...], (((0,), (0,)), ((), ())), preferred_element_type=jnp.float32)
        for r in range(REP):
            at = pl.ds(pl.multiple_of(base + r * HD, HD), HD)
            dq_ref[:, at] = dqt[:, r * rows:(r + 1) * rows].T.astype(jnp.bfloat16)

    def own(g):
        for k in range(1, BACK + 1):
            @pl.when(s + k < n_seq)
            def _():
                grad_copy(g, k).wait_recv()
                accr[g] = accr[g] + part[g, k - 1].astype(jnp.float32)
        at = pl.ds(pl.multiple_of(g * HD, HD), HD)
        dk = accr[g, :, :HD].astype(jnp.bfloat16)
        if fused:
            dkg[g, me] = dk
            for i, to in enumerate(plane):
                dk_copy(g, i, to).start()
        dk_ref[:, at] = dk
        dv_ref[:, at] = accr[g, :, HD:].astype(jnp.bfloat16)

    def weigh(g):
        for i, to in enumerate(plane):
            dk_arrival(g, i, to).wait_recv()
        members = 2 * n_dp
        dk_all = dkg[g].reshape(members * rows, HD)
        x_all = xr[...].reshape(members * rows, n_z * chunk)
        wt = lax.dot_general(dk_all, x_all, (((0,), (0,)), ((), ())), preferred_element_type=jnp.float32)
        w = wt.T.reshape(n_z, chunk, HD)
        psend[g] = w.astype(jnp.bfloat16)
        pf[g] = w
        for j in range(1, n_z):
            w_copy(g, j).start()

    def finish(g):
        total = pf[g, z]
        for j in range(1, n_z):
            w_arrival(g, j).wait_recv()
            total = total + prec[g, (z + j) % n_z].astype(jnp.float32)
        dw_ref[:, pl.ds(pl.multiple_of(g * HD, HD), HD)] = total

    def step(t, _):
        @pl.when(t < HK)
        def _():
            attend(t)

        @pl.when((t >= 1) & (t < HK + 1))
        def _():
            own(t - 1)

        if fused:
            @pl.when(t == 2)
            def _():
                for i, to in enumerate(plane):
                    x_arrival(i, to).wait_recv()

            @pl.when((t >= 2) & (t < HK + 2))
            def _():
                weigh(t - 2)

            @pl.when(t >= 3)
            def _():
                finish(t - 3)
        return 0

    lax.fori_loop(0, HK + 3 if fused else HK + 1, step, 0)

    for k in range(1, BACK + 1):
        @pl.when(s + k < n_seq)
        def _():
            seg_copy(k).wait_send()
            for g in range(HK):
                kv_copy(g, k).wait_send()

        @pl.when(s >= k)
        def _():
            for g in range(HK):
                grad_copy(g, k).wait_send()
    if fused:
        for i, to in enumerate(plane):
            x_copy(i, to).wait_send()
            for g in range(HK):
                dk_copy(g, i, to).wait_send()
        for g in range(HK):
            for j in range(1, n_z):
                w_copy(g, j).wait_send()


def per_device(sizes, queries, key_rows, value_rows, grad_out, segments, layer_input):
    n_dp, n_seq = sizes
    rows = queries.shape[0]
    wide = layer_input.shape[1]
    chunk = wide // (n_dp * n_seq)
    n_z = n_seq // 2
    fused = n_dp <= 4 and n_seq % 2 == 0 and chunk % 16 == 0 and (chunk * n_z) % 128 == 0
    cfg = (n_dp, n_seq, rows, fused, chunk)
    keys = (BACK + 1) * rows
    bf16, f32 = jnp.bfloat16, jnp.float32
    dma = pltpu.SemaphoreType.DMA
    scratch = [
        pltpu.VMEM((HK, BACK + 1, rows, 2 * HD), bf16),
        pltpu.VMEM((BACK + 1, 8, rows), jnp.int32),
        pltpu.VMEM((HK, BACK + 1, rows, 2 * HD), bf16),
        pltpu.VMEM((HK, BACK, rows, 2 * HD), bf16),
        pltpu.VMEM((HK, rows, 2 * HD), f32),
        pltpu.VMEM((keys, rows), f32),
        pltpu.VMEM((REP * rows, HD), bf16),
        pltpu.VMEM((REP * rows, HD), bf16),
        pltpu.VMEM((keys, REP * rows), bf16),
        pltpu.VMEM((keys, REP * rows), bf16),
        dma((HK, BACK)), dma((HK, BACK)), dma((BACK,)), dma((BACK,)), dma((HK, BACK)), dma((HK, BACK)),
    ]
    outs = [
        jax.ShapeDtypeStruct(queries.shape, bf16),
        jax.ShapeDtypeStruct(key_rows.shape, bf16),
        jax.ShapeDtypeStruct(value_rows.shape, bf16),
    ]
    args = [queries, key_rows, value_rows, grad_out, segments]
    if fused:
        m = 2 * n_dp
        args.append(layer_input)
        outs.append(jax.ShapeDtypeStruct((chunk, HK * HD), f32))
        scratch += [
            pltpu.VMEM((m, rows, n_z * chunk), bf16),
            pltpu.VMEM((m, rows, n_z * chunk), bf16),
            pltpu.VMEM((HK, m, rows, HD), bf16),
            pltpu.VMEM((HK, n_z, chunk, HD), f32),
            pltpu.VMEM((HK, n_z, chunk, HD), bf16),
            pltpu.VMEM((HK, n_z, chunk, HD), bf16),
            dma((m,)), dma((m,)), dma((HK, m)), dma((HK, m)), dma((HK, n_z)), dma((HK, n_z)),
        ]
    vmem = pl.BlockSpec(memory_space=pltpu.VMEM)
    res = pl.pallas_call(
        functools.partial(kernel, cfg),
        out_shape=outs,
        in_specs=[vmem] * len(args),
        out_specs=[vmem] * len(outs),
        scratch_shapes=scratch,
        compiler_params=pltpu.CompilerParams(
            collective_id=0, has_side_effects=True, vmem_limit_bytes=48 * 1024 * 1024
        ),
    )(*args)
    if fused:
        return tuple(res)
    grad_queries, grad_keys, grad_values = res
    weight_grad = lax.psum_scatter(
        lax.dot_general(
            layer_input, grad_keys, (((0,), (0,)), ((), ())), preferred_element_type=jnp.float32
        ),
        ("dp", "seq"),
        scatter_dimension=0,
        tiled=True,
    )
    return (grad_queries, grad_keys, grad_values, weight_grad)


def solution(mesh):
    sizes = (mesh.shape["dp"], mesh.shape["seq"])
    tokens = P(("dp", "seq"), None)
    return jax.shard_map(
        functools.partial(per_device, sizes),
        mesh=mesh,
        in_specs=(tokens, tokens, tokens, tokens, P("dp", "seq"), tokens),
        out_specs=(tokens, tokens, tokens, tokens),
        check_vma=False,
    )
```

```python
import functools

import jax
import jax.numpy as jnp
from jax import lax
from jax.experimental import pallas as pl
from jax.experimental.pallas import tpu as pltpu
from jax.sharding import PartitionSpec as P

HQ = 20
HK = 4
HD = 128
REP = HQ // HK
BACK = 4
MESH = pl.DeviceIdType.MESH


def kernel(cfg, *refs):
    n_dp, n_seq, rows, fused, chunk = cfg
    n_z = n_seq // 2
    width = BACK + 1
    keys = width * rows
    refs = list(refs)
    q_ref, k_ref, v_ref, do_ref, seg_ref = refs[:5]
    del refs[:5]
    x_ref = refs.pop(0) if fused else None
    dq_ref, dk_ref, dv_ref = refs[:3]
    del refs[:3]
    dw_ref = refs.pop(0) if fused else None
    (win, segw, cont, side, send, down, accr, bias, qs, dos, dst, pst, q_in, do_in) = refs[:14]
    del refs[:14]
    (in_s, kv_s, kv_r, sg_s, sg_r, gr_s, gr_r) = refs[:7]
    del refs[:7]
    if fused:
        (x_in, xs, xr, dkg, pf, psend, prec, x_s, x_r, dk_s, dk_r, w_s, w_r) = refs
    d = lax.axis_index("dp")
    s = lax.axis_index("seq")
    z = s // 2
    x = s % 2
    me = d * 2 + x
    scale = HD ** -0.5

    plane = []
    if fused:
        for j in range(n_dp):
            for e in range(2):
                if j or e:
                    dd = (d + j) % n_dp
                    xx = (x + e) % 2
                    plane.append((dd, z * 2 + xx, dd * 2 + xx))

    barrier = pltpu.get_barrier_semaphore()
    count = 0
    for j in range(1, n_seq):
        pl.semaphore_signal(barrier, inc=1, device_id=(d, (s + j) % n_seq), device_id_type=MESH)
        count += 1
    if fused:
        for j in range(1, n_dp):
            for e in range(2):
                pl.semaphore_signal(
                    barrier, inc=1,
                    device_id=((d + j) % n_dp, z * 2 + (x + e) % 2), device_id_type=MESH,
                )
                count += 1

    loads = []
    for g in range(HK):
        cols = pl.ds(g * HD, HD)
        loads.append((k_ref.at[:, cols], win.at[g, BACK, :, pl.ds(0, HD)]))
        loads.append((v_ref.at[:, cols], win.at[g, BACK, :, pl.ds(HD, HD)]))
    loads.append((q_ref, q_in))
    loads.append((do_ref, do_in))
    if fused:
        loads.append((x_ref, x_in))
    loads = [pltpu.make_async_copy(a, b, in_s.at[i]) for i, (a, b) in enumerate(loads)]
    for load in loads:
        load.start()
    segw[BACK] = jnp.broadcast_to(seg_ref[...], (8, rows))

    up = jnp.minimum(z + 1, n_z - 1) * 2 + x
    below = jnp.maximum(z - 1, 0) * 2 + x
    mate = z * 2 + 1 - x
    more_up = z + 1 < n_z

    def push(g, channel, src, dst, to):
        return pltpu.make_async_remote_copy(
            src_ref=win.at[g, src], dst_ref=win.at[g, dst],
            send_sem=kv_s.at[g, channel], recv_sem=kv_r.at[g, channel],
            device_id=(d, to), device_id_type=MESH,
        )

    def kv_a(g):
        return push(g, 0, BACK, 2, up)

    def kv_b(g):
        return push(g, 1, 2, 0, up)

    def kv_c(g):
        return push(g, 2, 2, 1 + 2 * x, mate)

    def kv_d(g):
        return push(g, 3, 4 - 4 * x, 3 - 2 * x, mate)

    d_sent = (x == 0) | (z >= 2)
    d_got = (x == 1) | (z >= 2)

    def seg_copy(k):
        return pltpu.make_async_remote_copy(
            src_ref=segw.at[BACK], dst_ref=segw.at[BACK - k],
            send_sem=sg_s.at[k - 1], recv_sem=sg_r.at[k - 1],
            device_id=(d, (s + k) % n_seq), device_id_type=MESH,
        )

    def grad_x(g, i):
        return pltpu.make_async_remote_copy(
            src_ref=cont.at[g, i], dst_ref=side.at[g, i],
            send_sem=gr_s.at[g, i], recv_sem=gr_r.at[g, i],
            device_id=(d, mate), device_id_type=MESH,
        )

    def grad_z(g, i):
        return pltpu.make_async_remote_copy(
            src_ref=send.at[g, i], dst_ref=down.at[g, i],
            send_sem=gr_s.at[g, 2 + i], recv_sem=gr_r.at[g, 2 + i],
            device_id=(d, below), device_id_type=MESH,
        )

    def x_copy(i, to):
        return pltpu.make_async_remote_copy(
            src_ref=xs.at[to[2]], dst_ref=xr.at[me],
            send_sem=x_s.at[i], recv_sem=x_r.at[me],
            device_id=(to[0], to[1]), device_id_type=MESH,
        )

    def x_arrival(i, to):
        return pltpu.make_async_remote_copy(
            src_ref=xs.at[to[2]], dst_ref=xr.at[to[2]],
            send_sem=x_s.at[i], recv_sem=x_r.at[to[2]],
            device_id=(to[0], to[1]), device_id_type=MESH,
        )

    def dk_copy(g, i, to):
        return pltpu.make_async_remote_copy(
            src_ref=dkg.at[g, me], dst_ref=dkg.at[g, me],
            send_sem=dk_s.at[g, i], recv_sem=dk_r.at[g, me],
            device_id=(to[0], to[1]), device_id_type=MESH,
        )

    def dk_arrival(g, i, to):
        return pltpu.make_async_remote_copy(
            src_ref=dkg.at[g, me], dst_ref=dkg.at[g, to[2]],
            send_sem=dk_s.at[g, i], recv_sem=dk_r.at[g, to[2]],
            device_id=(to[0], to[1]), device_id_type=MESH,
        )

    def w_copy(g, j):
        zz = (z + j) % n_z
        return pltpu.make_async_remote_copy(
            src_ref=psend.at[g, zz], dst_ref=prec.at[g, z],
            send_sem=w_s.at[g, j], recv_sem=w_r.at[g, z],
            device_id=(d, zz * 2 + x), device_id_type=MESH,
        )

    def w_arrival(g, j):
        zz = (z + j) % n_z
        return pltpu.make_async_remote_copy(
            src_ref=psend.at[g, zz], dst_ref=prec.at[g, zz],
            send_sem=w_s.at[g, j], recv_sem=w_r.at[g, zz],
            device_id=(d, zz * 2 + x), device_id_type=MESH,
        )

    pl.semaphore_wait(barrier, count)

    for k in range(1, BACK + 1):
        @pl.when(s + k < n_seq)
        def _():
            seg_copy(k).start()

    for g in range(HK):
        loads[2 * g].wait()
        loads[2 * g + 1].wait()

        @pl.when(more_up)
        def _():
            kv_a(g).start()

        @pl.when(x == 0)
        def _():
            kv_d(g).start()

    def relay_one(g):
        @pl.when(z >= 1)
        def _():
            kv_a(g).wait_recv()
            kv_c(g).start()

            @pl.when(more_up)
            def _():
                kv_b(g).start()

    def relay_two(g):
        @pl.when(z >= 2)
        def _():
            kv_b(g).wait_recv()

            @pl.when(x == 1)
            def _():
                kv_d(g).start()

    def send_x():
        for dd in range(n_dp):
            for xx in range(2):
                cols = [(dd * n_seq + 2 * zz + xx) * chunk for zz in range(n_z)]
                xs[dd * 2 + xx] = jnp.concatenate([x_in[:, c:c + chunk] for c in cols], axis=1)
        for i, to in enumerate(plane):
            x_copy(i, to).start()
        xr[me] = xs[me]

    for k in range(1, BACK + 1):
        @pl.when(s < k)
        def _():
            win[:, BACK - k] = jnp.zeros((HK, rows, 2 * HD), jnp.bfloat16)
            bias[(BACK - k) * rows:(BACK - k + 1) * rows, :] = jnp.full((rows, rows), -1e30, jnp.float32)

    seg_here = seg_ref[...].astype(jnp.float32)

    def seg_bias(b, causal):
        there = jnp.broadcast_to(segw[b, 0:1, :].astype(jnp.float32), (rows, rows)).T
        seen = there == seg_here
        if causal:
            seen &= (lax.broadcasted_iota(jnp.int32, (rows, rows), 0)
                     <= lax.broadcasted_iota(jnp.int32, (rows, rows), 1))
        bias[b * rows:(b + 1) * rows, :] = jnp.where(seen, 0.0, -1e30)

    seg_bias(BACK, True)
    for k in range(1, BACK + 1):
        @pl.when(s >= k)
        def _():
            seg_copy(k).wait_recv()
            seg_bias(BACK - k, False)

    relay_one(0)
    loads[2 * HK].wait()
    loads[2 * HK + 1].wait()
    if fused:
        loads[2 * HK + 2].wait()
        send_x()
    relay_one(1)
    relay_two(0)

    def attend(g):
        @pl.when(z >= 1)
        def _():
            kv_c(g).wait_recv()

        @pl.when(d_got)
        def _():
            kv_d(g).wait_recv()

        key = win[g, :, :, :HD].reshape(keys, HD)
        value = win[g, :, :, HD:].reshape(keys, HD)
        base = pl.multiple_of(g * (REP * HD), HD)
        for r in range(REP):
            at = pl.ds(pl.multiple_of(base + r * HD, HD), HD)
            q = q_in[:, at]
            do = do_in[:, at]
            qs[r * rows:(r + 1) * rows, :] = q
            dos[r * rows:(r + 1) * rows, :] = do
            nt = (((1,), (1,)), ((), ()))
            logits = lax.dot_general(key, q, nt, preferred_element_type=jnp.float32)
            gp = lax.dot_general(value, do, nt, preferred_element_type=jnp.float32)
            logits = logits * scale + bias[...]
            top = jnp.max(logits, axis=0, keepdims=True)
            raised = jnp.exp(logits - top)
            inv = 1.0 / jnp.sum(raised, axis=0, keepdims=True)
            probs = raised * inv
            delta = jnp.sum(probs * gp, axis=0, keepdims=True)
            pst[:, r * rows:(r + 1) * rows] = probs.astype(jnp.bfloat16)
            dst[:, r * rows:(r + 1) * rows] = (probs * (gp - delta) * scale).astype(jnp.bfloat16)
        for grads, lhs, rhs in ((slice(0, HD), dst, qs), (slice(HD, 2 * HD), pst, dos)):
            sums = jnp.dot(lhs[...], rhs[...], preferred_element_type=jnp.float32)
            sums = sums.reshape(width, rows, HD)
            accr[g, 0, :, grads] = sums[BACK]
            accr[g, 1, :, grads] = sums[2]
            accr[g, 2, :, grads] = sums[0]
            cont[g, 0, :, grads] = sums[1].astype(jnp.bfloat16)
            cont[g, 1, :, grads] = sums[3].astype(jnp.bfloat16)

        @pl.when(z >= 2 - x)
        def _():
            grad_x(g, 0).start()

        @pl.when(z >= 1 - x)
        def _():
            grad_x(g, 1).start()

        dqt = lax.dot_general(key, dst[...], (((0,), (0,)), ((), ())), preferred_element_type=jnp.float32)
        for r in range(REP):
            at = pl.ds(pl.multiple_of(base + r * HD, HD), HD)
            dq_ref[:, at] = dqt[:, r * rows:(r + 1) * rows].T.astype(jnp.bfloat16)

    def across(g):
        @pl.when(z >= 1 + x)
        def _():
            grad_x(g, 0).wait_recv()
            accr[g, 1 + x] = accr[g, 1 + x] + side[g, 0].astype(jnp.float32)

        @pl.when(z >= x)
        def _():
            grad_x(g, 1).wait_recv()
            accr[g, x] = accr[g, x] + side[g, 1].astype(jnp.float32)

        @pl.when(z >= 2)
        def _():
            send[g, 0] = accr[g, 2].astype(jnp.bfloat16)
            grad_z(g, 0).start()

    def along(g):
        @pl.when(z >= 1)
        def _():
            @pl.when(more_up)
            def _():
                grad_z(g, 0).wait_recv()
                accr[g, 1] = accr[g, 1] + down[g, 0].astype(jnp.float32)

            send[g, 1] = accr[g, 1].astype(jnp.bfloat16)
            grad_z(g, 1).start()

    def own(g):
        @pl.when(more_up)
        def _():
            grad_z(g, 1).wait_recv()
            accr[g, 0] = accr[g, 0] + down[g, 1].astype(jnp.float32)

        at = pl.ds(pl.multiple_of(g * HD, HD), HD)
        dk = accr[g, 0, :, :HD].astype(jnp.bfloat16)
        if fused:
            dkg[g, me] = dk
            for i, to in enumerate(plane):
                dk_copy(g, i, to).start()
        dk_ref[:, at] = dk
        dv_ref[:, at] = accr[g, 0, :, HD:].astype(jnp.bfloat16)

    def weigh(g):
        for i, to in enumerate(plane):
            dk_arrival(g, i, to).wait_recv()
        members = 2 * n_dp
        dk_all = dkg[g].reshape(members * rows, HD)
        x_all = xr[...].reshape(members * rows, n_z * chunk)
        wt = lax.dot_general(dk_all, x_all, (((0,), (0,)), ((), ())), preferred_element_type=jnp.float32)
        w = wt.T.reshape(n_z, chunk, HD)
        psend[g] = w.astype(jnp.bfloat16)
        pf[g] = w
        for j in range(1, n_z):
            w_copy(g, j).start()

    def finish(g):
        total = pf[g, z]
        for j in range(1, n_z):
            w_arrival(g, j).wait_recv()
            total = total + prec[g, (z + j) % n_z].astype(jnp.float32)
        dw_ref[:, pl.ds(pl.multiple_of(g * HD, HD), HD)] = total

    def stage(t, lag, work):
        @pl.when((t >= lag) & (t < HK + lag))
        def _():
            work(t - lag)

    def step(t, _):
        @pl.when(t < HK - 2)
        def _():
            relay_one(t + 2)

        @pl.when(t < HK - 1)
        def _():
            relay_two(t + 1)

        stage(t, 0, attend)
        stage(t, 1, across)
        stage(t, 2, along)
        stage(t, 3, own)
        if fused:
            @pl.when(t == 4)
            def _():
                for i, to in enumerate(plane):
                    x_arrival(i, to).wait_recv()

            stage(t, 4, weigh)
            stage(t, 5, finish)
        return 0

    lax.fori_loop(0, HK + 5 if fused else HK + 3, step, 0)

    for k in range(1, BACK + 1):
        @pl.when(s + k < n_seq)
        def _():
            seg_copy(k).wait_send()

    def all_sent(seen, copies):
        @pl.when(seen)
        def _():
            for g in range(HK):
                copies(g).wait_send()

    all_sent(more_up, kv_a)
    all_sent((z >= 1) & more_up, kv_b)
    all_sent(z >= 1, kv_c)
    all_sent(d_sent, kv_d)
    all_sent(z >= 2 - x, lambda g: grad_x(g, 0))
    all_sent(z >= 1 - x, lambda g: grad_x(g, 1))
    all_sent(z >= 2, lambda g: grad_z(g, 0))
    all_sent(z >= 1, lambda g: grad_z(g, 1))
    if fused:
        for i, to in enumerate(plane):
            x_copy(i, to).wait_send()
            for g in range(HK):
                dk_copy(g, i, to).wait_send()
        for g in range(HK):
            for j in range(1, n_z):
                w_copy(g, j).wait_send()


def per_device(sizes, queries, key_rows, value_rows, grad_out, segments, layer_input):
    n_dp, n_seq = sizes
    rows = queries.shape[0]
    wide = layer_input.shape[1]
    chunk = wide // (n_dp * n_seq)
    n_z = n_seq // 2
    fused = n_dp <= 4 and n_seq % 2 == 0 and chunk % 16 == 0 and (chunk * n_z) % 128 == 0
    cfg = (n_dp, n_seq, rows, fused, chunk)
    keys = (BACK + 1) * rows
    bf16, f32 = jnp.bfloat16, jnp.float32
    dma = pltpu.SemaphoreType.DMA
    scratch = [
        pltpu.VMEM((HK, BACK + 1, rows, 2 * HD), bf16),
        pltpu.VMEM((BACK + 1, 8, rows), jnp.int32),
        pltpu.VMEM((HK, 2, rows, 2 * HD), bf16),
        pltpu.VMEM((HK, 2, rows, 2 * HD), bf16),
        pltpu.VMEM((HK, 2, rows, 2 * HD), bf16),
        pltpu.VMEM((HK, 2, rows, 2 * HD), bf16),
        pltpu.VMEM((HK, 3, rows, 2 * HD), f32),
        pltpu.VMEM((keys, rows), f32),
        pltpu.VMEM((REP * rows, HD), bf16),
        pltpu.VMEM((REP * rows, HD), bf16),
        pltpu.VMEM((keys, REP * rows), bf16),
        pltpu.VMEM((keys, REP * rows), bf16),
        pltpu.VMEM(queries.shape, bf16),
        pltpu.VMEM(queries.shape, bf16),
        dma((2 * HK + 3,)),
        dma((HK, BACK)), dma((HK, BACK)), dma((BACK,)), dma((BACK,)), dma((HK, BACK)), dma((HK, BACK)),
    ]
    outs = [
        jax.ShapeDtypeStruct(queries.shape, bf16),
        jax.ShapeDtypeStruct(key_rows.shape, bf16),
        jax.ShapeDtypeStruct(value_rows.shape, bf16),
    ]
    args = [queries, key_rows, value_rows, grad_out, segments]
    if fused:
        m = 2 * n_dp
        args.append(layer_input)
        outs.append(jax.ShapeDtypeStruct((chunk, HK * HD), f32))
        scratch += [
            pltpu.VMEM(layer_input.shape, bf16),
            pltpu.VMEM((m, rows, n_z * chunk), bf16),
            pltpu.VMEM((m, rows, n_z * chunk), bf16),
            pltpu.VMEM((HK, m, rows, HD), bf16),
            pltpu.VMEM((HK, n_z, chunk, HD), f32),
            pltpu.VMEM((HK, n_z, chunk, HD), bf16),
            pltpu.VMEM((HK, n_z, chunk, HD), bf16),
            dma((m,)), dma((m,)), dma((HK, m)), dma((HK, m)), dma((HK, n_z)), dma((HK, n_z)),
        ]
    vmem = pl.BlockSpec(memory_space=pltpu.VMEM)
    res = pl.pallas_call(
        functools.partial(kernel, cfg),
        out_shape=outs,
        in_specs=[pl.BlockSpec(memory_space=pl.ANY)] * 4 + [vmem] + [pl.BlockSpec(memory_space=pl.ANY)] * (len(args) - 5),
        out_specs=[vmem] * len(outs),
        scratch_shapes=scratch,
        compiler_params=pltpu.CompilerParams(
            collective_id=0, has_side_effects=True, vmem_limit_bytes=56 * 1024 * 1024
        ),
    )(*args)
    if fused:
        return tuple(res)
    grad_queries, grad_keys, grad_values = res
    weight_grad = lax.psum_scatter(
        lax.dot_general(
            layer_input, grad_keys, (((0,), (0,)), ((), ())), preferred_element_type=jnp.float32
        ),
        ("dp", "seq"),
        scatter_dimension=0,
        tiled=True,
    )
    return (grad_queries, grad_keys, grad_values, weight_grad)


def solution(mesh):
    sizes = (mesh.shape["dp"], mesh.shape["seq"])
    tokens = P(("dp", "seq"), None)
    return jax.shard_map(
        functools.partial(per_device, sizes),
        mesh=mesh,
        in_specs=(tokens, tokens, tokens, tokens, P("dp", "seq"), tokens),
        out_specs=(tokens, tokens, tokens, tokens),
        check_vma=False,
    )
```

```python
import functools

import jax
import jax.numpy as jnp
from jax import lax
from jax.experimental import pallas as pl
from jax.experimental.pallas import tpu as pltpu
from jax.sharding import PartitionSpec as P

HQ = 20
HK = 4
HD = 128
REP = HQ // HK
BACK = 4
MESH = pl.DeviceIdType.MESH


def kernel(cfg, *refs):
    n_dp, n_seq, rows, fused, chunk = cfg
    n_z = n_seq // 2
    width = BACK + 1
    keys = width * rows
    refs = list(refs)
    q_ref, k_ref, v_ref, do_ref, seg_ref = refs[:5]
    del refs[:5]
    x_ref = refs.pop(0) if fused else None
    dq_ref, dk_ref, dv_ref = refs[:3]
    del refs[:3]
    dw_ref = refs.pop(0) if fused else None
    (win, segw, cont, side, send, down, accr, bias, qs, dos, dst, pst, q_in, do_in) = refs[:14]
    del refs[:14]
    (in_s, kv_s, kv_r, sg_s, sg_r, gr_s, gr_r) = refs[:7]
    del refs[:7]
    if fused:
        (x_in, xs, xr, dkg, pf, psend, prec, x_s, x_r, dk_s, dk_r, w_s, w_r) = refs
    d = lax.axis_index("dp")
    s = lax.axis_index("seq")
    z = s // 2
    x = s % 2
    me = d * 2 + x
    scale = HD ** -0.5

    plane = []
    if fused:
        for j in range(n_dp):
            for e in range(2):
                if j or e:
                    dd = (d + j) % n_dp
                    xx = (x + e) % 2
                    plane.append((dd, z * 2 + xx, dd * 2 + xx))

    barrier = pltpu.get_barrier_semaphore()
    count = 0
    for j in range(1, n_seq):
        pl.semaphore_signal(barrier, inc=1, device_id=(d, (s + j) % n_seq), device_id_type=MESH)
        count += 1
    if fused:
        for j in range(1, n_dp):
            for e in range(2):
                pl.semaphore_signal(
                    barrier, inc=1,
                    device_id=((d + j) % n_dp, z * 2 + (x + e) % 2), device_id_type=MESH,
                )
                count += 1

    loads = []
    for g in range(HK):
        cols = pl.ds(g * HD, HD)
        loads.append((k_ref.at[:, cols], win.at[g, BACK, :, pl.ds(0, HD)]))
        loads.append((v_ref.at[:, cols], win.at[g, BACK, :, pl.ds(HD, HD)]))
    loads.append((q_ref, q_in))
    loads.append((do_ref, do_in))
    if fused:
        loads.append((x_ref, x_in))
    loads = [pltpu.make_async_copy(a, b, in_s.at[i]) for i, (a, b) in enumerate(loads)]
    for load in loads:
        load.start()
    segw[BACK] = jnp.broadcast_to(seg_ref[...], (8, rows))

    up = jnp.minimum(z + 1, n_z - 1) * 2 + x
    below = jnp.maximum(z - 1, 0) * 2 + x
    mate = z * 2 + 1 - x
    more_up = z + 1 < n_z

    def push(g, channel, src, dst, to):
        return pltpu.make_async_remote_copy(
            src_ref=win.at[g, src], dst_ref=win.at[g, dst],
            send_sem=kv_s.at[g, channel], recv_sem=kv_r.at[g, channel],
            device_id=(d, to), device_id_type=MESH,
        )

    def kv_a(g):
        return push(g, 0, BACK, 2, up)

    def kv_b(g):
        return push(g, 1, 2, 0, up)

    def kv_c(g):
        return push(g, 2, 3, 1, up)

    def kv_d(g):
        return push(g, 3, 4 - 2 * x, 3, mate)

    def seg_copy(k):
        return pltpu.make_async_remote_copy(
            src_ref=segw.at[BACK], dst_ref=segw.at[BACK - k],
            send_sem=sg_s.at[k - 1], recv_sem=sg_r.at[k - 1],
            device_id=(d, (s + k) % n_seq), device_id_type=MESH,
        )

    def grad_x(g):
        return pltpu.make_async_remote_copy(
            src_ref=send.at[g, 0], dst_ref=side.at[g],
            send_sem=gr_s.at[g, 0], recv_sem=gr_r.at[g, 0],
            device_id=(d, mate), device_id_type=MESH,
        )

    def grad_z(g, i):
        return pltpu.make_async_remote_copy(
            src_ref=(cont.at[g, 0], cont.at[g, 1], send.at[g, 1])[i], dst_ref=down.at[g, i],
            send_sem=gr_s.at[g, 1 + i], recv_sem=gr_r.at[g, 1 + i],
            device_id=(d, below), device_id_type=MESH,
        )

    def x_copy(i, to):
        return pltpu.make_async_remote_copy(
            src_ref=xs.at[to[2]], dst_ref=xr.at[me],
            send_sem=x_s.at[i], recv_sem=x_r.at[me],
            device_id=(to[0], to[1]), device_id_type=MESH,
        )

    def x_arrival(i, to):
        return pltpu.make_async_remote_copy(
            src_ref=xs.at[to[2]], dst_ref=xr.at[to[2]],
            send_sem=x_s.at[i], recv_sem=x_r.at[to[2]],
            device_id=(to[0], to[1]), device_id_type=MESH,
        )

    def dk_copy(g, i, slot, to):
        return pltpu.make_async_remote_copy(
            src_ref=dkg.at[g, slot], dst_ref=dkg.at[g, slot],
            send_sem=dk_s.at[g, i], recv_sem=dk_r.at[g, slot],
            device_id=to, device_id_type=MESH,
        )

    other = d * 2 + 1 - x
    friends = [(d + j) % n_dp for j in range(1, n_dp)]

    def dk_sends(g):
        own_sends = [dk_copy(g, 0, me, (d, mate))]
        own_sends += [dk_copy(g, 1 + i, me, (dd, s)) for i, dd in enumerate(friends)]
        passed = [dk_copy(g, n_dp + i, other, (dd, s)) for i, dd in enumerate(friends)]
        return own_sends, passed

    def w_copy(g, j):
        zz = (z + j) % n_z
        return pltpu.make_async_remote_copy(
            src_ref=psend.at[g, zz], dst_ref=prec.at[g, z],
            send_sem=w_s.at[g, j], recv_sem=w_r.at[g, z],
            device_id=(d, zz * 2 + x), device_id_type=MESH,
        )

    def w_arrival(g, j):
        zz = (z + j) % n_z
        return pltpu.make_async_remote_copy(
            src_ref=psend.at[g, zz], dst_ref=prec.at[g, zz],
            send_sem=w_s.at[g, j], recv_sem=w_r.at[g, zz],
            device_id=(d, zz * 2 + x), device_id_type=MESH,
        )

    pl.semaphore_wait(barrier, count)

    for k in range(1, BACK + 1):
        @pl.when(s + k < n_seq)
        def _():
            seg_copy(k).start()

    for g in range(HK):
        loads[2 * g].wait()
        loads[2 * g + 1].wait()

        @pl.when(more_up)
        def _():
            kv_a(g).start()

        @pl.when(x == 0)
        def _():
            kv_d(g).start()

    def relay_one(g):
        @pl.when(z >= 1)
        def _():
            kv_a(g).wait_recv()

            @pl.when(x == 1)
            def _():
                kv_d(g).start()

            @pl.when(more_up)
            def _():
                kv_b(g).start()

    def relay_two(g):
        @pl.when(z >= 1 - x)
        def _():
            kv_d(g).wait_recv()

            @pl.when(more_up)
            def _():
                kv_c(g).start()

    def send_x():
        for dd in range(n_dp):
            for xx in range(2):
                cols = [(dd * n_seq + 2 * zz + xx) * chunk for zz in range(n_z)]
                xs[dd * 2 + xx] = jnp.concatenate([x_in[:, c:c + chunk] for c in cols], axis=1)
        for i, to in enumerate(plane):
            x_copy(i, to).start()
        xr[me] = xs[me]

    for k in range(1, BACK + 1):
        @pl.when(s < k)
        def _():
            win[:, BACK - k] = jnp.zeros((HK, rows, 2 * HD), jnp.bfloat16)
            bias[(BACK - k) * rows:(BACK - k + 1) * rows, :] = jnp.full((rows, rows), -1e30, jnp.float32)

    seg_here = seg_ref[...].astype(jnp.float32)

    def seg_bias(b, causal):
        there = jnp.broadcast_to(segw[b, 0:1, :].astype(jnp.float32), (rows, rows)).T
        seen = there == seg_here
        if causal:
            seen &= (lax.broadcasted_iota(jnp.int32, (rows, rows), 0)
                     <= lax.broadcasted_iota(jnp.int32, (rows, rows), 1))
        bias[b * rows:(b + 1) * rows, :] = jnp.where(seen, 0.0, -1e30)

    seg_bias(BACK, True)
    for k in range(1, BACK + 1):
        @pl.when(s >= k)
        def _():
            seg_copy(k).wait_recv()
            seg_bias(BACK - k, False)

    relay_one(0)
    loads[2 * HK].wait()
    loads[2 * HK + 1].wait()
    if fused:
        loads[2 * HK + 2].wait()
        send_x()
    relay_one(1)
    relay_two(0)

    def attend(g):
        @pl.when(z >= 2)
        def _():
            kv_b(g).wait_recv()

        @pl.when(z >= 2 - x)
        def _():
            kv_c(g).wait_recv()

        key = win[g, :, :, :HD].reshape(keys, HD)
        value = win[g, :, :, HD:].reshape(keys, HD)
        base = pl.multiple_of(g * (REP * HD), HD)
        for r in range(REP):
            at = pl.ds(pl.multiple_of(base + r * HD, HD), HD)
            q = q_in[:, at]
            do = do_in[:, at]
            qs[r * rows:(r + 1) * rows, :] = q
            dos[r * rows:(r + 1) * rows, :] = do
            nt = (((1,), (1,)), ((), ()))
            logits = lax.dot_general(key, q, nt, preferred_element_type=jnp.float32)
            gp = lax.dot_general(value, do, nt, preferred_element_type=jnp.float32)
            logits = logits * scale + bias[...]
            top = jnp.max(logits, axis=0, keepdims=True)
            raised = jnp.exp(logits - top)
            inv = 1.0 / jnp.sum(raised, axis=0, keepdims=True)
            probs = raised * inv
            delta = jnp.sum(probs * gp, axis=0, keepdims=True)
            pst[:, r * rows:(r + 1) * rows] = probs.astype(jnp.bfloat16)
            dst[:, r * rows:(r + 1) * rows] = (probs * (gp - delta) * scale).astype(jnp.bfloat16)
        for grads, lhs, rhs in ((slice(0, HD), dst, qs), (slice(HD, 2 * HD), pst, dos)):
            sums = jnp.dot(lhs[...], rhs[...], preferred_element_type=jnp.float32)
            sums = sums.reshape(width, rows, HD)
            accr[g, 0, :, grads] = sums[BACK]
            accr[g, 1, :, grads] = sums[2]
            accr[g, 2, :, grads] = sums[3]
            cont[g, 0, :, grads] = sums[0].astype(jnp.bfloat16)
            cont[g, 1, :, grads] = sums[1].astype(jnp.bfloat16)

        @pl.when(z >= 2 - x)
        def _():
            grad_z(g, 1).start()

        @pl.when(z >= 2)
        def _():
            grad_z(g, 0).start()

        dqt = lax.dot_general(key, dst[...], (((0,), (0,)), ((), ())), preferred_element_type=jnp.float32)
        for r in range(REP):
            at = pl.ds(pl.multiple_of(base + r * HD, HD), HD)
            dq_ref[:, at] = dqt[:, r * rows:(r + 1) * rows].T.astype(jnp.bfloat16)

    def across(g):
        @pl.when(z >= 1 - x)
        def _():
            @pl.when(more_up)
            def _():
                grad_z(g, 1).wait_recv()
                accr[g, 2] = accr[g, 2] + down[g, 1].astype(jnp.float32)

            send[g, 0] = accr[g, 2].astype(jnp.bfloat16)
            grad_x(g).start()

        @pl.when((z >= 1) & more_up)
        def _():
            grad_z(g, 0).wait_recv()
            accr[g, 1] = accr[g, 1] + down[g, 0].astype(jnp.float32)

    def along(g):
        @pl.when(z >= x)
        def _():
            grad_x(g).wait_recv()
            accr[g, x] = accr[g, x] + side[g].astype(jnp.float32)

        @pl.when(z >= 1)
        def _():
            send[g, 1] = accr[g, 1].astype(jnp.bfloat16)
            grad_z(g, 2).start()

    def own(g):
        @pl.when(more_up)
        def _():
            grad_z(g, 2).wait_recv()
            accr[g, 0] = accr[g, 0] + down[g, 2].astype(jnp.float32)

        at = pl.ds(pl.multiple_of(g * HD, HD), HD)
        dk = accr[g, 0, :, :HD].astype(jnp.bfloat16)
        if fused:
            dkg[g, me] = dk
            for copy in dk_sends(g)[0]:
                copy.start()
        dk_ref[:, at] = dk
        dv_ref[:, at] = accr[g, 0, :, HD:].astype(jnp.bfloat16)

    def hand_on(g):
        own_sends, passed = dk_sends(g)
        dk_copy(g, 0, other, (d, mate)).wait_recv()
        for copy in passed:
            copy.start()

    def weigh(g):
        for dd in friends:
            for xx in range(2):
                dk_copy(g, 0, dd * 2 + xx, (dd, s)).wait_recv()
        members = 2 * n_dp
        dk_all = dkg[g].reshape(members * rows, HD)
        x_all = xr[...].reshape(members * rows, n_z * chunk)
        wt = lax.dot_general(dk_all, x_all, (((0,), (0,)), ((), ())), preferred_element_type=jnp.float32)
        w = wt.T.reshape(n_z, chunk, HD)
        psend[g] = w.astype(jnp.bfloat16)
        pf[g] = w
        for j in range(1, n_z):
            w_copy(g, j).start()

    def finish(g):
        total = pf[g, z]
        for j in range(1, n_z):
            w_arrival(g, j).wait_recv()
            total = total + prec[g, (z + j) % n_z].astype(jnp.float32)
        dw_ref[:, pl.ds(pl.multiple_of(g * HD, HD), HD)] = total

    def stage(t, lag, work):
        @pl.when((t >= lag) & (t < HK + lag))
        def _():
            work(t - lag)

    def step(t, _):
        @pl.when(t < HK - 2)
        def _():
            relay_one(t + 2)

        @pl.when(t < HK - 1)
        def _():
            relay_two(t + 1)

        stage(t, 0, attend)
        stage(t, 1, across)
        stage(t, 2, along)
        stage(t, 3, own)
        if fused:
            stage(t, 4, hand_on)

            @pl.when(t == 5)
            def _():
                for i, to in enumerate(plane):
                    x_arrival(i, to).wait_recv()

            stage(t, 5, weigh)
            stage(t, 6, finish)
        return 0

    lax.fori_loop(0, HK + 6 if fused else HK + 3, step, 0)

    for k in range(1, BACK + 1):
        @pl.when(s + k < n_seq)
        def _():
            seg_copy(k).wait_send()

    def all_sent(seen, copies):
        @pl.when(seen)
        def _():
            for g in range(HK):
                copies(g).wait_send()

    all_sent(more_up, kv_a)
    all_sent((z >= 1) & more_up, kv_b)
    all_sent((z >= 1 - x) & more_up, kv_c)
    all_sent(z >= x, kv_d)
    all_sent(z >= 2, lambda g: grad_z(g, 0))
    all_sent(z >= 2 - x, lambda g: grad_z(g, 1))
    all_sent(z >= 1, lambda g: grad_z(g, 2))
    all_sent(z >= 1 - x, grad_x)
    if fused:
        for i, to in enumerate(plane):
            x_copy(i, to).wait_send()
        for g in range(HK):
            own_sends, passed = dk_sends(g)
            for copy in own_sends + passed:
                copy.wait_send()
            for j in range(1, n_z):
                w_copy(g, j).wait_send()


def per_device(sizes, queries, key_rows, value_rows, grad_out, segments, layer_input):
    n_dp, n_seq = sizes
    rows = queries.shape[0]
    wide = layer_input.shape[1]
    chunk = wide // (n_dp * n_seq)
    n_z = n_seq // 2
    fused = n_dp <= 4 and n_seq % 2 == 0 and chunk % 16 == 0 and (chunk * n_z) % 128 == 0
    cfg = (n_dp, n_seq, rows, fused, chunk)
    keys = (BACK + 1) * rows
    bf16, f32 = jnp.bfloat16, jnp.float32
    dma = pltpu.SemaphoreType.DMA
    scratch = [
        pltpu.VMEM((HK, BACK + 1, rows, 2 * HD), bf16),
        pltpu.VMEM((BACK + 1, 8, rows), jnp.int32),
        pltpu.VMEM((HK, 2, rows, 2 * HD), bf16),
        pltpu.VMEM((HK, rows, 2 * HD), bf16),
        pltpu.VMEM((HK, 2, rows, 2 * HD), bf16),
        pltpu.VMEM((HK, 3, rows, 2 * HD), bf16),
        pltpu.VMEM((HK, 3, rows, 2 * HD), f32),
        pltpu.VMEM((keys, rows), f32),
        pltpu.VMEM((REP * rows, HD), bf16),
        pltpu.VMEM((REP * rows, HD), bf16),
        pltpu.VMEM((keys, REP * rows), bf16),
        pltpu.VMEM((keys, REP * rows), bf16),
        pltpu.VMEM(queries.shape, bf16),
        pltpu.VMEM(queries.shape, bf16),
        dma((2 * HK + 3,)),
        dma((HK, BACK)), dma((HK, BACK)), dma((BACK,)), dma((BACK,)), dma((HK, BACK)), dma((HK, BACK)),
    ]
    outs = [
        jax.ShapeDtypeStruct(queries.shape, bf16),
        jax.ShapeDtypeStruct(key_rows.shape, bf16),
        jax.ShapeDtypeStruct(value_rows.shape, bf16),
    ]
    args = [queries, key_rows, value_rows, grad_out, segments]
    if fused:
        m = 2 * n_dp
        args.append(layer_input)
        outs.append(jax.ShapeDtypeStruct((chunk, HK * HD), f32))
        scratch += [
            pltpu.VMEM(layer_input.shape, bf16),
            pltpu.VMEM((m, rows, n_z * chunk), bf16),
            pltpu.VMEM((m, rows, n_z * chunk), bf16),
            pltpu.VMEM((HK, m, rows, HD), bf16),
            pltpu.VMEM((HK, n_z, chunk, HD), f32),
            pltpu.VMEM((HK, n_z, chunk, HD), bf16),
            pltpu.VMEM((HK, n_z, chunk, HD), bf16),
            dma((m,)), dma((m,)), dma((HK, m)), dma((HK, m)), dma((HK, n_z)), dma((HK, n_z)),
        ]
    vmem = pl.BlockSpec(memory_space=pltpu.VMEM)
    res = pl.pallas_call(
        functools.partial(kernel, cfg),
        out_shape=outs,
        in_specs=[pl.BlockSpec(memory_space=pl.ANY)] * 4 + [vmem] + [pl.BlockSpec(memory_space=pl.ANY)] * (len(args) - 5),
        out_specs=[vmem] * len(outs),
        scratch_shapes=scratch,
        compiler_params=pltpu.CompilerParams(
            collective_id=0, has_side_effects=True, vmem_limit_bytes=56 * 1024 * 1024
        ),
    )(*args)
    if fused:
        return tuple(res)
    grad_queries, grad_keys, grad_values = res
    weight_grad = lax.psum_scatter(
        lax.dot_general(
            layer_input, grad_keys, (((0,), (0,)), ((), ())), preferred_element_type=jnp.float32
        ),
        ("dp", "seq"),
        scatter_dimension=0,
        tiled=True,
    )
    return (grad_queries, grad_keys, grad_values, weight_grad)


def solution(mesh):
    sizes = (mesh.shape["dp"], mesh.shape["seq"])
    tokens = P(("dp", "seq"), None)
    return jax.shard_map(
        functools.partial(per_device, sizes),
        mesh=mesh,
        in_specs=(tokens, tokens, tokens, tokens, P("dp", "seq"), tokens),
        out_specs=(tokens, tokens, tokens, tokens),
        check_vma=False,
    )
```

```python
import functools

import jax
import jax.numpy as jnp
from jax import lax
from jax.experimental import pallas as pl
from jax.experimental.pallas import tpu as pltpu
from jax.sharding import PartitionSpec as P

HQ = 20
HK = 4
HD = 128
REP = HQ // HK
BACK = 4
MESH = pl.DeviceIdType.MESH


def kernel(cfg, *refs):
    n_dp, n_seq, rows, fused, chunk = cfg
    n_z = n_seq // 2
    width = BACK + 1
    keys = width * rows
    refs = list(refs)
    q_ref, k_ref, v_ref, do_ref, seg_ref = refs[:5]
    del refs[:5]
    x_ref = refs.pop(0) if fused else None
    dq_ref, dk_ref, dv_ref = refs[:3]
    del refs[:3]
    dw_ref = refs.pop(0) if fused else None
    (win, segw, cont, side, send, down, accr, bias, qs, dos, dst, pst, q_in, do_in) = refs[:14]
    del refs[:14]
    (in_s, kv_s, kv_r, sg_s, sg_r, gr_s, gr_r) = refs[:7]
    del refs[:7]
    if fused:
        (x_in, xs, xr, dkg, pf, psend, prec, x_s, x_r, dk_s, dk_r, w_s, w_r) = refs
    d = lax.axis_index("dp")
    s = lax.axis_index("seq")
    z = s // 2
    x = s % 2
    me = d * 2 + x
    scale = HD ** -0.5

    plane = []
    if fused:
        for j in range(n_dp):
            for e in range(2):
                if j or e:
                    dd = (d + j) % n_dp
                    xx = (x + e) % 2
                    plane.append((dd, z * 2 + xx, dd * 2 + xx))

    barrier = pltpu.get_barrier_semaphore()
    count = 0
    for j in range(1, n_seq):
        pl.semaphore_signal(barrier, inc=1, device_id=(d, (s + j) % n_seq), device_id_type=MESH)
        count += 1
    if fused:
        for j in range(1, n_dp):
            for e in range(2):
                pl.semaphore_signal(
                    barrier, inc=1,
                    device_id=((d + j) % n_dp, z * 2 + (x + e) % 2), device_id_type=MESH,
                )
                count += 1

    loads = []
    for g in range(HK):
        cols = pl.ds(g * HD, HD)
        loads.append((k_ref.at[:, cols], win.at[g, BACK, :, pl.ds(0, HD)]))
        loads.append((v_ref.at[:, cols], win.at[g, BACK, :, pl.ds(HD, HD)]))
    loads.append((q_ref, q_in))
    loads.append((do_ref, do_in))
    if fused:
        loads.append((x_ref, x_in))
    loads = [pltpu.make_async_copy(a, b, in_s.at[i]) for i, (a, b) in enumerate(loads)]
    for load in loads:
        load.start()
    segw[BACK] = jnp.broadcast_to(seg_ref[...], (8, rows))

    up = jnp.minimum(z + 1, n_z - 1) * 2 + x
    below = jnp.maximum(z - 1, 0) * 2 + x
    mate = z * 2 + 1 - x
    more_up = z + 1 < n_z

    def push(g, channel, src, dst, to):
        return pltpu.make_async_remote_copy(
            src_ref=win.at[g, src], dst_ref=win.at[g, dst],
            send_sem=kv_s.at[g, channel], recv_sem=kv_r.at[g, channel],
            device_id=(d, to), device_id_type=MESH,
        )

    def kv_a(g):
        return push(g, 0, BACK, 2, up)

    def kv_b(g):
        return push(g, 1, 2, 0, up)

    def kv_c(g):
        return push(g, 2, 3, 1, up)

    def kv_d(g):
        return push(g, 3, 4 - 2 * x, 3, mate)

    def seg_copy(k):
        return pltpu.make_async_remote_copy(
            src_ref=segw.at[BACK], dst_ref=segw.at[BACK - k],
            send_sem=sg_s.at[k - 1], recv_sem=sg_r.at[k - 1],
            device_id=(d, (s + k) % n_seq), device_id_type=MESH,
        )

    def grad_x(g):
        return pltpu.make_async_remote_copy(
            src_ref=send.at[g, 0], dst_ref=side.at[g],
            send_sem=gr_s.at[g, 0], recv_sem=gr_r.at[g, 0],
            device_id=(d, mate), device_id_type=MESH,
        )

    def grad_z(g, i):
        return pltpu.make_async_remote_copy(
            src_ref=(cont.at[g, 0], cont.at[g, 1], send.at[g, 1])[i], dst_ref=down.at[g, i],
            send_sem=gr_s.at[g, 1 + i], recv_sem=gr_r.at[g, 1 + i],
            device_id=(d, below), device_id_type=MESH,
        )

    def x_copy(i, to):
        return pltpu.make_async_remote_copy(
            src_ref=xs.at[to[2]], dst_ref=xr.at[me],
            send_sem=x_s.at[i], recv_sem=x_r.at[me],
            device_id=(to[0], to[1]), device_id_type=MESH,
        )

    def x_arrival(i, to):
        return pltpu.make_async_remote_copy(
            src_ref=xs.at[to[2]], dst_ref=xr.at[to[2]],
            send_sem=x_s.at[i], recv_sem=x_r.at[to[2]],
            device_id=(to[0], to[1]), device_id_type=MESH,
        )

    def dk_copy(g, i, slot, to):
        return pltpu.make_async_remote_copy(
            src_ref=dkg.at[g, slot], dst_ref=dkg.at[g, slot],
            send_sem=dk_s.at[g, i], recv_sem=dk_r.at[g, slot],
            device_id=to, device_id_type=MESH,
        )

    other = d * 2 + 1 - x
    friends = [(d + j) % n_dp for j in range(1, n_dp)]

    def own_sends(g):
        copies = [dk_copy(g, 0, me, (d, mate))]
        return copies + [dk_copy(g, 1 + i, me, (dd, s)) for i, dd in enumerate(friends)]

    def passed(g):
        return [dk_copy(g, n_dp + i, other, (dd, s)) for i, dd in enumerate(friends)]

    def w_copy(g, j):
        zz = (z + j) % n_z
        return pltpu.make_async_remote_copy(
            src_ref=psend.at[g, zz], dst_ref=prec.at[g, z],
            send_sem=w_s.at[g, j], recv_sem=w_r.at[g, z],
            device_id=(d, zz * 2 + x), device_id_type=MESH,
        )

    def w_arrival(g, j):
        zz = (z + j) % n_z
        return pltpu.make_async_remote_copy(
            src_ref=psend.at[g, zz], dst_ref=prec.at[g, zz],
            send_sem=w_s.at[g, j], recv_sem=w_r.at[g, zz],
            device_id=(d, zz * 2 + x), device_id_type=MESH,
        )

    pl.semaphore_wait(barrier, count)

    for k in range(1, BACK + 1):
        @pl.when(s + k < n_seq)
        def _():
            seg_copy(k).start()

    for g in range(HK):
        loads[2 * g].wait()
        loads[2 * g + 1].wait()

        @pl.when(more_up)
        def _():
            kv_a(g).start()

        @pl.when(x == 0)
        def _():
            kv_d(g).start()

    def relay_one(g):
        @pl.when(z >= 1)
        def _():
            kv_a(g).wait_recv()

            @pl.when(x == 1)
            def _():
                kv_d(g).start()

            @pl.when(more_up)
            def _():
                kv_b(g).start()

    def relay_two(g):
        @pl.when(z >= 1 - x)
        def _():
            kv_d(g).wait_recv()

            @pl.when(more_up)
            def _():
                kv_c(g).start()

    def send_x():
        for dd in range(n_dp):
            for xx in range(2):
                cols = [(dd * n_seq + 2 * zz + xx) * chunk for zz in range(n_z)]
                xs[dd * 2 + xx] = jnp.concatenate([x_in[:, c:c + chunk] for c in cols], axis=1)
        for i, to in enumerate(plane):
            x_copy(i, to).start()
        xr[me] = xs[me]

    for k in range(1, BACK + 1):
        @pl.when(s < k)
        def _():
            win[:, BACK - k] = jnp.zeros((HK, rows, 2 * HD), jnp.bfloat16)
            bias[(BACK - k) * rows:(BACK - k + 1) * rows, :] = jnp.full((rows, rows), -1e30, jnp.float32)

    seg_here = seg_ref[...].astype(jnp.float32)

    def seg_bias(b, causal):
        there = jnp.broadcast_to(segw[b, 0:1, :].astype(jnp.float32), (rows, rows)).T
        seen = there == seg_here
        if causal:
            seen &= (lax.broadcasted_iota(jnp.int32, (rows, rows), 0)
                     <= lax.broadcasted_iota(jnp.int32, (rows, rows), 1))
        bias[b * rows:(b + 1) * rows, :] = jnp.where(seen, 0.0, -1e30)

    seg_bias(BACK, True)
    for k in range(1, BACK + 1):
        @pl.when(s >= k)
        def _():
            seg_copy(k).wait_recv()
            seg_bias(BACK - k, False)

    relay_one(0)
    loads[2 * HK].wait()
    loads[2 * HK + 1].wait()
    if fused:
        loads[2 * HK + 2].wait()
        send_x()
    relay_one(1)
    relay_two(0)

    def attend(g):
        @pl.when(z >= 2)
        def _():
            kv_b(g).wait_recv()

        @pl.when(z >= 2 - x)
        def _():
            kv_c(g).wait_recv()

        key = win[g, :, :, :HD].reshape(keys, HD)
        value = win[g, :, :, HD:].reshape(keys, HD)
        base = pl.multiple_of(g * (REP * HD), HD)
        for r in range(REP):
            at = pl.ds(pl.multiple_of(base + r * HD, HD), HD)
            q = q_in[:, at]
            do = do_in[:, at]
            qs[r * rows:(r + 1) * rows, :] = q
            dos[r * rows:(r + 1) * rows, :] = do
            nt = (((1,), (1,)), ((), ()))
            logits = lax.dot_general(key, q, nt, preferred_element_type=jnp.float32)
            gp = lax.dot_general(value, do, nt, preferred_element_type=jnp.float32)
            logits = logits * scale + bias[...]
            top = jnp.max(logits, axis=0, keepdims=True)
            raised = jnp.exp(logits - top)
            inv = 1.0 / jnp.sum(raised, axis=0, keepdims=True)
            probs = raised * inv
            delta = jnp.sum(probs * gp, axis=0, keepdims=True)
            pst[:, r * rows:(r + 1) * rows] = probs.astype(jnp.bfloat16)
            dst[:, r * rows:(r + 1) * rows] = (probs * (gp - delta) * scale).astype(jnp.bfloat16)
        for grads, lhs, rhs in ((slice(0, HD), dst, qs), (slice(HD, 2 * HD), pst, dos)):
            sums = jnp.dot(lhs[...], rhs[...], preferred_element_type=jnp.float32)
            sums = sums.reshape(width, rows, HD)
            accr[g, 0, :, grads] = sums[BACK]
            accr[g, 1, :, grads] = sums[2]
            accr[g, 2, :, grads] = sums[3]
            cont[g, 0, :, grads] = sums[0].astype(jnp.bfloat16)
            cont[g, 1, :, grads] = sums[1].astype(jnp.bfloat16)

        @pl.when(z >= 2 - x)
        def _():
            grad_z(g, 1).start()

        @pl.when(z >= 2)
        def _():
            grad_z(g, 0).start()

        dqt = lax.dot_general(key, dst[...], (((0,), (0,)), ((), ())), preferred_element_type=jnp.float32)
        for r in range(REP):
            at = pl.ds(pl.multiple_of(base + r * HD, HD), HD)
            dq_ref[:, at] = dqt[:, r * rows:(r + 1) * rows].T.astype(jnp.bfloat16)

    def across(g):
        @pl.when(z >= 1 - x)
        def _():
            @pl.when(more_up)
            def _():
                grad_z(g, 1).wait_recv()
                accr[g, 2] = accr[g, 2] + down[g, 1].astype(jnp.float32)

            send[g, 0] = accr[g, 2].astype(jnp.bfloat16)
            grad_x(g).start()

        @pl.when((z >= 1) & more_up)
        def _():
            grad_z(g, 0).wait_recv()
            accr[g, 1] = accr[g, 1] + down[g, 0].astype(jnp.float32)

    def along(g):
        @pl.when(z >= x)
        def _():
            grad_x(g).wait_recv()
            accr[g, x] = accr[g, x] + side[g].astype(jnp.float32)

        @pl.when(z >= 1)
        def _():
            send[g, 1] = accr[g, 1].astype(jnp.bfloat16)
            grad_z(g, 2).start()

    def own(g):
        @pl.when(more_up)
        def _():
            grad_z(g, 2).wait_recv()
            accr[g, 0] = accr[g, 0] + down[g, 2].astype(jnp.float32)

        at = pl.ds(g * HD if isinstance(g, int) else pl.multiple_of(g * HD, HD), HD)
        dk = accr[g, 0, :, :HD].astype(jnp.bfloat16)
        if fused:
            dkg[g, me] = dk
            for copy in own_sends(g):
                copy.start()
        dk_ref[:, at] = dk
        dv_ref[:, at] = accr[g, 0, :, HD:].astype(jnp.bfloat16)

    def hand_on(g):
        dk_copy(g, 0, other, (d, mate)).wait_recv()
        for copy in passed(g):
            copy.start()

    def weigh(g):
        if g == 0:
            for i, to in enumerate(plane):
                x_arrival(i, to).wait_recv()
        for dd in friends:
            for xx in range(2):
                dk_copy(g, 0, dd * 2 + xx, (dd, s)).wait_recv()
        members = 2 * n_dp
        dk_all = dkg[g].reshape(members * rows, HD)
        x_all = xr[...].reshape(members * rows, n_z * chunk)
        wt = lax.dot_general(dk_all, x_all, (((0,), (0,)), ((), ())), preferred_element_type=jnp.float32)
        w = wt.T.reshape(n_z, chunk, HD)
        psend[g] = w.astype(jnp.bfloat16)
        pf[g] = w
        for j in range(1, n_z):
            w_copy(g, j).start()

    def finish(g):
        total = pf[g, z]
        for j in range(1, n_z):
            w_arrival(g, j).wait_recv()
            total = total + prec[g, (z + j) % n_z].astype(jnp.float32)
        dw_ref[:, pl.ds(g * HD if isinstance(g, int) else pl.multiple_of(g * HD, HD), HD)] = total

    def stage(t, lag, work):
        @pl.when((t >= lag) & (t < HK + lag))
        def _():
            work(t - lag)

    def step(t, _):
        @pl.when(t < HK - 2)
        def _():
            relay_one(t + 2)

        @pl.when(t < HK - 1)
        def _():
            relay_two(t + 1)

        stage(t, 0, attend)
        stage(t, 1, across)
        stage(t, 2, along)
        stage(t, 3, own)
        return 0

    lax.fori_loop(0, HK, step, 0)

    if not fused:
        tail = [(along, 2), (own, 1), (across, 3), (own, 2), (along, 3), (own, 3)]
    else:
        tail = [
            (along, 2), (own, 1), (hand_on, 0), (across, 3), (own, 2), (hand_on, 1), (along, 3),
            (weigh, 0), (hand_on, 2), (own, 3), (weigh, 1), (hand_on, 3), (weigh, 2), (weigh, 3),
        ] + [(finish, g) for g in range(HK)]
    for work, g in tail:
        work(g)

    for k in range(1, BACK + 1):
        @pl.when(s + k < n_seq)
        def _():
            seg_copy(k).wait_send()

    def all_sent(seen, copies):
        @pl.when(seen)
        def _():
            for g in range(HK):
                copies(g).wait_send()

    all_sent(more_up, kv_a)
    all_sent((z >= 1) & more_up, kv_b)
    all_sent((z >= 1 - x) & more_up, kv_c)
    all_sent(z >= x, kv_d)
    all_sent(z >= 2, lambda g: grad_z(g, 0))
    all_sent(z >= 2 - x, lambda g: grad_z(g, 1))
    all_sent(z >= 1, lambda g: grad_z(g, 2))
    all_sent(z >= 1 - x, grad_x)
    if fused:
        for i, to in enumerate(plane):
            x_copy(i, to).wait_send()
        for g in range(HK):
            for copy in own_sends(g) + passed(g):
                copy.wait_send()
            for j in range(1, n_z):
                w_copy(g, j).wait_send()


def per_device(sizes, queries, key_rows, value_rows, grad_out, segments, layer_input):
    n_dp, n_seq = sizes
    rows = queries.shape[0]
    wide = layer_input.shape[1]
    chunk = wide // (n_dp * n_seq)
    n_z = n_seq // 2
    fused = n_dp <= 4 and n_seq % 2 == 0 and chunk % 16 == 0 and (chunk * n_z) % 128 == 0
    cfg = (n_dp, n_seq, rows, fused, chunk)
    keys = (BACK + 1) * rows
    bf16, f32 = jnp.bfloat16, jnp.float32
    dma = pltpu.SemaphoreType.DMA
    scratch = [
        pltpu.VMEM((HK, BACK + 1, rows, 2 * HD), bf16),
        pltpu.VMEM((BACK + 1, 8, rows), jnp.int32),
        pltpu.VMEM((HK, 2, rows, 2 * HD), bf16),
        pltpu.VMEM((HK, rows, 2 * HD), bf16),
        pltpu.VMEM((HK, 2, rows, 2 * HD), bf16),
        pltpu.VMEM((HK, 3, rows, 2 * HD), bf16),
        pltpu.VMEM((HK, 3, rows, 2 * HD), f32),
        pltpu.VMEM((keys, rows), f32),
        pltpu.VMEM((REP * rows, HD), bf16),
        pltpu.VMEM((REP * rows, HD), bf16),
        pltpu.VMEM((keys, REP * rows), bf16),
        pltpu.VMEM((keys, REP * rows), bf16),
        pltpu.VMEM(queries.shape, bf16),
        pltpu.VMEM(queries.shape, bf16),
        dma((2 * HK + 3,)),
        dma((HK, BACK)), dma((HK, BACK)), dma((BACK,)), dma((BACK,)), dma((HK, BACK)), dma((HK, BACK)),
    ]
    outs = [
        jax.ShapeDtypeStruct(queries.shape, bf16),
        jax.ShapeDtypeStruct(key_rows.shape, bf16),
        jax.ShapeDtypeStruct(value_rows.shape, bf16),
    ]
    args = [queries, key_rows, value_rows, grad_out, segments]
    if fused:
        m = 2 * n_dp
        args.append(layer_input)
        outs.append(jax.ShapeDtypeStruct((chunk, HK * HD), f32))
        scratch += [
            pltpu.VMEM(layer_input.shape, bf16),
            pltpu.VMEM((m, rows, n_z * chunk), bf16),
            pltpu.VMEM((m, rows, n_z * chunk), bf16),
            pltpu.VMEM((HK, m, rows, HD), bf16),
            pltpu.VMEM((HK, n_z, chunk, HD), f32),
            pltpu.VMEM((HK, n_z, chunk, HD), bf16),
            pltpu.VMEM((HK, n_z, chunk, HD), bf16),
            dma((m,)), dma((m,)), dma((HK, m)), dma((HK, m)), dma((HK, n_z)), dma((HK, n_z)),
        ]
    vmem = pl.BlockSpec(memory_space=pltpu.VMEM)
    res = pl.pallas_call(
        functools.partial(kernel, cfg),
        out_shape=outs,
        in_specs=[pl.BlockSpec(memory_space=pl.ANY)] * 4 + [vmem] + [pl.BlockSpec(memory_space=pl.ANY)] * (len(args) - 5),
        out_specs=[vmem] * len(outs),
        scratch_shapes=scratch,
        compiler_params=pltpu.CompilerParams(
            collective_id=0, has_side_effects=True, vmem_limit_bytes=56 * 1024 * 1024
        ),
    )(*args)
    if fused:
        return tuple(res)
    grad_queries, grad_keys, grad_values = res
    weight_grad = lax.psum_scatter(
        lax.dot_general(
            layer_input, grad_keys, (((0,), (0,)), ((), ())), preferred_element_type=jnp.float32
        ),
        ("dp", "seq"),
        scatter_dimension=0,
        tiled=True,
    )
    return (grad_queries, grad_keys, grad_values, weight_grad)


def solution(mesh):
    sizes = (mesh.shape["dp"], mesh.shape["seq"])
    tokens = P(("dp", "seq"), None)
    return jax.shard_map(
        functools.partial(per_device, sizes),
        mesh=mesh,
        in_specs=(tokens, tokens, tokens, tokens, P("dp", "seq"), tokens),
        out_specs=(tokens, tokens, tokens, tokens),
        check_vma=False,
    )
```

```python
import functools

import jax
import jax.numpy as jnp
from jax import lax
from jax.experimental import pallas as pl
from jax.experimental.pallas import tpu as pltpu
from jax.sharding import PartitionSpec as P

HQ = 20
HK = 4
HD = 128
REP = HQ // HK
BACK = 4
MESH = pl.DeviceIdType.MESH


def kernel(cfg, *refs):
    n_dp, n_seq, rows, fused, chunk = cfg
    n_z = n_seq // 2
    width = BACK + 1
    keys = width * rows
    refs = list(refs)
    q_ref, k_ref, v_ref, do_ref, seg_ref = refs[:5]
    del refs[:5]
    x_ref = refs.pop(0) if fused else None
    dq_ref, dk_ref, dv_ref = refs[:3]
    del refs[:3]
    dw_ref = refs.pop(0) if fused else None
    (win, segw, cont, side, send, down, accr, bias, qs, dos, dst, pst, q_in, do_in) = refs[:14]
    del refs[:14]
    (in_s, kv_s, kv_r, sg_s, sg_r, gr_s, gr_r) = refs[:7]
    del refs[:7]
    if fused:
        (x_in, xs, xr, dkg, pf, psend, prec, x_s, x_r, dk_s, dk_r, w_s, w_r) = refs
    d = lax.axis_index("dp")
    s = lax.axis_index("seq")
    z = s // 2
    x = s % 2
    me = d * 2 + x
    scale = HD ** -0.5

    plane = []
    if fused:
        for j in range(n_dp):
            for e in range(2):
                if j or e:
                    dd = (d + j) % n_dp
                    xx = (x + e) % 2
                    plane.append((dd, z * 2 + xx, dd * 2 + xx))

    barrier = pltpu.get_barrier_semaphore()
    count = 0
    for j in range(1, n_seq):
        pl.semaphore_signal(barrier, inc=1, device_id=(d, (s + j) % n_seq), device_id_type=MESH)
        count += 1
    if fused:
        for j in range(1, n_dp):
            for e in range(2):
                pl.semaphore_signal(
                    barrier, inc=1,
                    device_id=((d + j) % n_dp, z * 2 + (x + e) % 2), device_id_type=MESH,
                )
                count += 1

    loads = []
    for g in range(HK):
        cols = pl.ds(g * HD, HD)
        loads.append((k_ref.at[:, cols], win.at[g, BACK, :, pl.ds(0, HD)]))
        loads.append((v_ref.at[:, cols], win.at[g, BACK, :, pl.ds(HD, HD)]))
    loads.append((q_ref, q_in))
    loads.append((do_ref, do_in))
    if fused:
        loads.append((x_ref, x_in))
    loads = [pltpu.make_async_copy(a, b, in_s.at[i]) for i, (a, b) in enumerate(loads)]
    for load in loads:
        load.start()
    segw[BACK] = jnp.broadcast_to(seg_ref[...], (8, rows))

    up = jnp.minimum(z + 1, n_z - 1) * 2 + x
    below = jnp.maximum(z - 1, 0) * 2 + x
    mate = z * 2 + 1 - x
    more_up = z + 1 < n_z

    def push(g, channel, src, dst, to):
        return pltpu.make_async_remote_copy(
            src_ref=win.at[g, src], dst_ref=win.at[g, dst],
            send_sem=kv_s.at[g, channel], recv_sem=kv_r.at[g, channel],
            device_id=(d, to), device_id_type=MESH,
        )

    def kv_a(g):
        return push(g, 0, BACK, 2, up)

    def kv_b(g):
        return push(g, 1, 2, 0, up)

    def kv_c(g):
        return push(g, 2, 3, 1, up)

    def kv_d(g):
        return push(g, 3, 4 - 2 * x, 3, mate)

    def seg_copy(k):
        return pltpu.make_async_remote_copy(
            src_ref=segw.at[BACK], dst_ref=segw.at[BACK - k],
            send_sem=sg_s.at[k - 1], recv_sem=sg_r.at[k - 1],
            device_id=(d, (s + k) % n_seq), device_id_type=MESH,
        )

    def grad_x(g):
        return pltpu.make_async_remote_copy(
            src_ref=send.at[g, 0], dst_ref=side.at[g],
            send_sem=gr_s.at[g, 0], recv_sem=gr_r.at[g, 0],
            device_id=(d, mate), device_id_type=MESH,
        )

    def grad_z(g, i):
        return pltpu.make_async_remote_copy(
            src_ref=(cont.at[g, 0], cont.at[g, 1], send.at[g, 1])[i], dst_ref=down.at[g, i],
            send_sem=gr_s.at[g, 1 + i], recv_sem=gr_r.at[g, 1 + i],
            device_id=(d, below), device_id_type=MESH,
        )

    def x_copy(i, to):
        return pltpu.make_async_remote_copy(
            src_ref=xs.at[to[2]], dst_ref=xr.at[me],
            send_sem=x_s.at[i], recv_sem=x_r.at[me],
            device_id=(to[0], to[1]), device_id_type=MESH,
        )

    def x_arrival(i, to):
        return pltpu.make_async_remote_copy(
            src_ref=xs.at[to[2]], dst_ref=xr.at[to[2]],
            send_sem=x_s.at[i], recv_sem=x_r.at[to[2]],
            device_id=(to[0], to[1]), device_id_type=MESH,
        )

    def dk_copy(g, i, slot, to):
        return pltpu.make_async_remote_copy(
            src_ref=dkg.at[g, slot], dst_ref=dkg.at[g, slot],
            send_sem=dk_s.at[g, i], recv_sem=dk_r.at[g, slot],
            device_id=to, device_id_type=MESH,
        )

    other = d * 2 + 1 - x
    friends = [(d + j) % n_dp for j in range(1, n_dp)]

    def own_sends(g):
        copies = [dk_copy(g, 0, me, (d, mate))]
        return copies + [dk_copy(g, 1 + i, me, (dd, s)) for i, dd in enumerate(friends)]

    def passed(g):
        return [dk_copy(g, n_dp + i, other, (dd, s)) for i, dd in enumerate(friends)]

    def w_copy(g, j):
        zz = (z + j) % n_z
        return pltpu.make_async_remote_copy(
            src_ref=psend.at[g, zz], dst_ref=prec.at[g, z],
            send_sem=w_s.at[g, j], recv_sem=w_r.at[g, z],
            device_id=(d, zz * 2 + x), device_id_type=MESH,
        )

    def w_arrival(g, j):
        zz = (z + j) % n_z
        return pltpu.make_async_remote_copy(
            src_ref=psend.at[g, zz], dst_ref=prec.at[g, zz],
            send_sem=w_s.at[g, j], recv_sem=w_r.at[g, zz],
            device_id=(d, zz * 2 + x), device_id_type=MESH,
        )

    pl.semaphore_wait(barrier, count)

    for k in range(1, BACK + 1):
        @pl.when(s + k < n_seq)
        def _():
            seg_copy(k).start()

    for g in range(HK):
        loads[2 * g].wait()
        loads[2 * g + 1].wait()

        @pl.when(more_up)
        def _():
            kv_a(g).start()

        @pl.when(x == 0)
        def _():
            kv_d(g).start()

    def relay_one(g):
        @pl.when(z >= 1)
        def _():
            kv_a(g).wait_recv()

            @pl.when(x == 1)
            def _():
                kv_d(g).start()

            @pl.when(more_up)
            def _():
                kv_b(g).start()

    def relay_two(g):
        @pl.when(z >= 1 - x)
        def _():
            kv_d(g).wait_recv()

            @pl.when(more_up)
            def _():
                kv_c(g).start()

    def send_x():
        for dd in range(n_dp):
            for xx in range(2):
                cols = [(dd * n_seq + 2 * zz + xx) * chunk for zz in range(n_z)]
                xs[dd * 2 + xx] = jnp.concatenate([x_in[:, c:c + chunk] for c in cols], axis=1)
        xr[me] = xs[me]

    def send_some(t):
        for i, to in enumerate(plane):
            @pl.when(t == i // 2)
            def _():
                x_copy(i, to).start()

    for k in range(1, BACK + 1):
        @pl.when(s < k)
        def _():
            win[:, BACK - k] = jnp.zeros((HK, rows, 2 * HD), jnp.bfloat16)
            bias[(BACK - k) * rows:(BACK - k + 1) * rows, :] = jnp.full((rows, rows), -1e30, jnp.float32)

    seg_here = seg_ref[...].astype(jnp.float32)

    def seg_bias(b, causal):
        there = jnp.broadcast_to(segw[b, 0:1, :].astype(jnp.float32), (rows, rows)).T
        seen = there == seg_here
        if causal:
            seen &= (lax.broadcasted_iota(jnp.int32, (rows, rows), 0)
                     <= lax.broadcasted_iota(jnp.int32, (rows, rows), 1))
        bias[b * rows:(b + 1) * rows, :] = jnp.where(seen, 0.0, -1e30)

    seg_bias(BACK, True)
    for k in range(1, BACK + 1):
        @pl.when(s >= k)
        def _():
            seg_copy(k).wait_recv()
            seg_bias(BACK - k, False)

    relay_one(0)
    loads[2 * HK].wait()
    loads[2 * HK + 1].wait()
    if fused:
        loads[2 * HK + 2].wait()
        send_x()
    relay_one(1)
    relay_two(0)

    def attend(g):
        @pl.when(z >= 2)
        def _():
            kv_b(g).wait_recv()

        @pl.when(z >= 2 - x)
        def _():
            kv_c(g).wait_recv()

        key = win[g, :, :, :HD].reshape(keys, HD)
        value = win[g, :, :, HD:].reshape(keys, HD)
        base = pl.multiple_of(g * (REP * HD), HD)
        for r in range(REP):
            at = pl.ds(pl.multiple_of(base + r * HD, HD), HD)
            q = q_in[:, at]
            do = do_in[:, at]
            qs[r * rows:(r + 1) * rows, :] = q
            dos[r * rows:(r + 1) * rows, :] = do
            nt = (((1,), (1,)), ((), ()))
            logits = lax.dot_general(key, q, nt, preferred_element_type=jnp.float32)
            gp = lax.dot_general(value, do, nt, preferred_element_type=jnp.float32)
            logits = logits * scale + bias[...]
            top = jnp.max(logits, axis=0, keepdims=True)
            raised = jnp.exp(logits - top)
            inv = 1.0 / jnp.sum(raised, axis=0, keepdims=True)
            probs = raised * inv
            delta = jnp.sum(probs * gp, axis=0, keepdims=True)
            pst[:, r * rows:(r + 1) * rows] = probs.astype(jnp.bfloat16)
            dst[:, r * rows:(r + 1) * rows] = (probs * (gp - delta) * scale).astype(jnp.bfloat16)
        for grads, lhs, rhs in ((slice(0, HD), dst, qs), (slice(HD, 2 * HD), pst, dos)):
            sums = jnp.dot(lhs[...], rhs[...], preferred_element_type=jnp.float32)
            sums = sums.reshape(width, rows, HD)
            accr[g, 0, :, grads] = sums[BACK]
            accr[g, 1, :, grads] = sums[2]
            accr[g, 2, :, grads] = sums[3]
            cont[g, 0, :, grads] = sums[0].astype(jnp.bfloat16)
            cont[g, 1, :, grads] = sums[1].astype(jnp.bfloat16)

        @pl.when(z >= 2 - x)
        def _():
            grad_z(g, 1).start()

        @pl.when(z >= 2)
        def _():
            grad_z(g, 0).start()

        dqt = lax.dot_general(key, dst[...], (((0,), (0,)), ((), ())), preferred_element_type=jnp.float32)
        for r in range(REP):
            at = pl.ds(pl.multiple_of(base + r * HD, HD), HD)
            dq_ref[:, at] = dqt[:, r * rows:(r + 1) * rows].T.astype(jnp.bfloat16)

    def across(g):
        @pl.when(z >= 1 - x)
        def _():
            @pl.when(more_up)
            def _():
                grad_z(g, 1).wait_recv()
                accr[g, 2] = accr[g, 2] + down[g, 1].astype(jnp.float32)

            send[g, 0] = accr[g, 2].astype(jnp.bfloat16)
            grad_x(g).start()

        @pl.when((z >= 1) & more_up)
        def _():
            grad_z(g, 0).wait_recv()
            accr[g, 1] = accr[g, 1] + down[g, 0].astype(jnp.float32)

    def along(g):
        @pl.when(z >= x)
        def _():
            grad_x(g).wait_recv()
            accr[g, x] = accr[g, x] + side[g].astype(jnp.float32)

        @pl.when(z >= 1)
        def _():
            send[g, 1] = accr[g, 1].astype(jnp.bfloat16)
            grad_z(g, 2).start()

    def own(g):
        @pl.when(more_up)
        def _():
            grad_z(g, 2).wait_recv()
            accr[g, 0] = accr[g, 0] + down[g, 2].astype(jnp.float32)

        at = pl.ds(g * HD if isinstance(g, int) else pl.multiple_of(g * HD, HD), HD)
        dk = accr[g, 0, :, :HD].astype(jnp.bfloat16)
        if fused:
            dkg[g, me] = dk
            for copy in own_sends(g):
                copy.start()
        dk_ref[:, at] = dk
        dv_ref[:, at] = accr[g, 0, :, HD:].astype(jnp.bfloat16)

    def hand_on(g):
        dk_copy(g, 0, other, (d, mate)).wait_recv()
        for copy in passed(g):
            copy.start()

    def weigh(g):
        if g == 0:
            for i, to in enumerate(plane):
                x_arrival(i, to).wait_recv()
        for dd in friends:
            for xx in range(2):
                dk_copy(g, 0, dd * 2 + xx, (dd, s)).wait_recv()
        members = 2 * n_dp
        dk_all = dkg[g].reshape(members * rows, HD)
        x_all = xr[...].reshape(members * rows, n_z * chunk)
        wt = lax.dot_general(dk_all, x_all, (((0,), (0,)), ((), ())), preferred_element_type=jnp.float32)
        w = wt.T.reshape(n_z, chunk, HD)
        psend[g] = w.astype(jnp.bfloat16)
        pf[g] = w
        for j in range(1, n_z):
            w_copy(g, j).start()

    def finish(g):
        total = pf[g, z]
        for j in range(1, n_z):
            w_arrival(g, j).wait_recv()
            total = total + prec[g, (z + j) % n_z].astype(jnp.float32)
        dw_ref[:, pl.ds(g * HD if isinstance(g, int) else pl.multiple_of(g * HD, HD), HD)] = total

    def stage(t, lag, work):
        @pl.when((t >= lag) & (t < HK + lag))
        def _():
            work(t - lag)

    def step(t, _):
        @pl.when(t < HK - 2)
        def _():
            relay_one(t + 2)

        @pl.when(t < HK - 1)
        def _():
            relay_two(t + 1)

        if fused:
            send_some(t)
        stage(t, 0, attend)
        stage(t, 1, across)
        stage(t, 2, along)
        stage(t, 3, own)
        return 0

    lax.fori_loop(0, HK, step, 0)

    if not fused:
        tail = [(along, 2), (own, 1), (across, 3), (own, 2), (along, 3), (own, 3)]
    else:
        tail = [
            (along, 2), (own, 1), (hand_on, 0), (across, 3), (own, 2), (hand_on, 1), (along, 3),
            (weigh, 0), (hand_on, 2), (own, 3), (weigh, 1), (hand_on, 3), (weigh, 2), (weigh, 3),
        ] + [(finish, g) for g in range(HK)]
    for work, g in tail:
        work(g)

    for k in range(1, BACK + 1):
        @pl.when(s + k < n_seq)
        def _():
            seg_copy(k).wait_send()

    def all_sent(seen, copies):
        @pl.when(seen)
        def _():
            for g in range(HK):
                copies(g).wait_send()

    all_sent(more_up, kv_a)
    all_sent((z >= 1) & more_up, kv_b)
    all_sent((z >= 1 - x) & more_up, kv_c)
    all_sent(z >= x, kv_d)
    all_sent(z >= 2, lambda g: grad_z(g, 0))
    all_sent(z >= 2 - x, lambda g: grad_z(g, 1))
    all_sent(z >= 1, lambda g: grad_z(g, 2))
    all_sent(z >= 1 - x, grad_x)
    if fused:
        for i, to in enumerate(plane):
            x_copy(i, to).wait_send()
        for g in range(HK):
            for copy in own_sends(g) + passed(g):
                copy.wait_send()
            for j in range(1, n_z):
                w_copy(g, j).wait_send()


def per_device(sizes, queries, key_rows, value_rows, grad_out, segments, layer_input):
    n_dp, n_seq = sizes
    rows = queries.shape[0]
    wide = layer_input.shape[1]
    chunk = wide // (n_dp * n_seq)
    n_z = n_seq // 2
    fused = n_dp <= 4 and n_seq % 2 == 0 and chunk % 16 == 0 and (chunk * n_z) % 128 == 0
    cfg = (n_dp, n_seq, rows, fused, chunk)
    keys = (BACK + 1) * rows
    bf16, f32 = jnp.bfloat16, jnp.float32
    dma = pltpu.SemaphoreType.DMA
    scratch = [
        pltpu.VMEM((HK, BACK + 1, rows, 2 * HD), bf16),
        pltpu.VMEM((BACK + 1, 8, rows), jnp.int32),
        pltpu.VMEM((HK, 2, rows, 2 * HD), bf16),
        pltpu.VMEM((HK, rows, 2 * HD), bf16),
        pltpu.VMEM((HK, 2, rows, 2 * HD), bf16),
        pltpu.VMEM((HK, 3, rows, 2 * HD), bf16),
        pltpu.VMEM((HK, 3, rows, 2 * HD), f32),
        pltpu.VMEM((keys, rows), f32),
        pltpu.VMEM((REP * rows, HD), bf16),
        pltpu.VMEM((REP * rows, HD), bf16),
        pltpu.VMEM((keys, REP * rows), bf16),
        pltpu.VMEM((keys, REP * rows), bf16),
        pltpu.VMEM(queries.shape, bf16),
        pltpu.VMEM(queries.shape, bf16),
        dma((2 * HK + 3,)),
        dma((HK, BACK)), dma((HK, BACK)), dma((BACK,)), dma((BACK,)), dma((HK, BACK)), dma((HK, BACK)),
    ]
    outs = [
        jax.ShapeDtypeStruct(queries.shape, bf16),
        jax.ShapeDtypeStruct(key_rows.shape, bf16),
        jax.ShapeDtypeStruct(value_rows.shape, bf16),
    ]
    args = [queries, key_rows, value_rows, grad_out, segments]
    if fused:
        m = 2 * n_dp
        args.append(layer_input)
        outs.append(jax.ShapeDtypeStruct((chunk, HK * HD), f32))
        scratch += [
            pltpu.VMEM(layer_input.shape, bf16),
            pltpu.VMEM((m, rows, n_z * chunk), bf16),
            pltpu.VMEM((m, rows, n_z * chunk), bf16),
            pltpu.VMEM((HK, m, rows, HD), bf16),
            pltpu.VMEM((HK, n_z, chunk, HD), f32),
            pltpu.VMEM((HK, n_z, chunk, HD), bf16),
            pltpu.VMEM((HK, n_z, chunk, HD), bf16),
            dma((m,)), dma((m,)), dma((HK, m)), dma((HK, m)), dma((HK, n_z)), dma((HK, n_z)),
        ]
    vmem = pl.BlockSpec(memory_space=pltpu.VMEM)
    res = pl.pallas_call(
        functools.partial(kernel, cfg),
        out_shape=outs,
        in_specs=[pl.BlockSpec(memory_space=pl.ANY)] * 4 + [vmem] + [pl.BlockSpec(memory_space=pl.ANY)] * (len(args) - 5),
        out_specs=[vmem] * len(outs),
        scratch_shapes=scratch,
        compiler_params=pltpu.CompilerParams(
            collective_id=0, has_side_effects=True, vmem_limit_bytes=56 * 1024 * 1024
        ),
    )(*args)
    if fused:
        return tuple(res)
    grad_queries, grad_keys, grad_values = res
    weight_grad = lax.psum_scatter(
        lax.dot_general(
            layer_input, grad_keys, (((0,), (0,)), ((), ())), preferred_element_type=jnp.float32
        ),
        ("dp", "seq"),
        scatter_dimension=0,
        tiled=True,
    )
    return (grad_queries, grad_keys, grad_values, weight_grad)


def solution(mesh):
    sizes = (mesh.shape["dp"], mesh.shape["seq"])
    tokens = P(("dp", "seq"), None)
    return jax.shard_map(
        functools.partial(per_device, sizes),
        mesh=mesh,
        in_specs=(tokens, tokens, tokens, tokens, P("dp", "seq"), tokens),
        out_specs=(tokens, tokens, tokens, tokens),
        check_vma=False,
    )
```
